256 devices in a mesh: dp: 16 (over y, x), mem: 16 (over z, core).
Axes of the slice: x: 4, y: 4, z: 8, core: 2. Of those that a mesh axis runs over, the one named last changes fastest.
Arguments:
- tokens: bfloat16 [131072, 2048], P(('dp', 'mem')), may hold values from -320 to 320
- q_weight: bfloat16 [2048, 1024], replicated, may hold values from -0.13 to 0.13
- memory_keys: bfloat16 [16, 64, 128, 512], P('dp', 'mem'), may hold values from -45 to 45
- memory_values: bfloat16 [16, 64, 128, 512], P('dp', 'mem'), may hold values from -6 to 6
- retrieved_block_index: int32 [16, 16, 8], P('dp', 'mem'), may hold values from 0 to 63, as said below
- d_context: bfloat16 [131072, 1024], P(('dp', 'mem')), may hold values from -6 to 6
Outputs:
- context: bfloat16 [131072, 1024], P(('dp', 'mem'))
- grad_tokens: bfloat16 [131072, 2048], P(('dp', 'mem'))
- grad_q_weight: float32 [2048, 1024], P(('dp', 'mem'))
The draws below stay inside these ranges and needn't reach their ends.
Inputs may be any that keep to these rules, and one draw needn't show every extreme that they name: `retrieved_block_index`: A segment's 8 ids are distinct; at most 2 of them lie in one memory shard (ids k * 4 to (k + 1) * 4 - 1), and in every segment exactly three shards hold 2 of them.
All inputs are finite; a program needn't handle non-finite values.
Results may differ from the reference program's by a relative error of at most 0.015.
Values may be sent and summed in bfloat16 or wider, within the bound.
A program may use at most 128 MiB of HBM per device.

```python
import jax
import jax.numpy as jnp
from jax import lax

D = 2048
KVH = 4
HD = 128
SEG = 512
BLOCK = 128
TOPB = 8
MB_DEV = 4
GRP = 2
QW = 1024
KVW = 512
SEGS = 16
BLOCKS = 64
ROWS = 131072
N_DP = 16
N_MEM = 16


def shared_weight(key):
    return jnp.clip(jax.random.normal(key, (D, QW), jnp.float32) * D ** (-0.5), -0.13, 0.13)


def draw_q_weight(key, part):
    return shared_weight(key).astype(jnp.bfloat16)


def draw_tokens(key, part):
    key = jax.random.fold_in(key, 1)
    k_base, k_scale = jax.random.split(key, 2)
    base = jnp.clip(jax.random.normal(k_base, (ROWS, D), jnp.float32), -6.0, 6.0)
    segments = ROWS // SEG
    width = D // segments
    paired = jax.random.permutation(k_scale, segments)
    row_block = jnp.arange(ROWS) // SEG
    col_block = jnp.arange(D) // width
    boost = jnp.where(paired[row_block][:, None] == col_block[None, :], 4.0, 1.0)
    values = base * boost
    return values.astype(jnp.bfloat16)


def draw_memory_keys(key, part):
    key = jax.random.fold_in(key, 2)
    k_base = jax.random.fold_in(key, 0)
    shape = (N_DP, BLOCKS, BLOCK, KVW)
    values = jnp.clip(jax.random.normal(k_base, shape, jnp.float32) * 2.5, -15.0, 15.0)
    return values.astype(jnp.bfloat16)


def draw_retrieved_block_index(key, part):
    key = jax.random.fold_in(key, 3)
    k_hot, k_score, k_first, k_step, k_order = jax.random.split(key, 5)
    popular_block_rank = jax.vmap(lambda item: jax.random.permutation(item, N_MEM))(jax.random.split(k_hot, N_DP))
    score_boost_extra = jnp.maximum(0, 3 - popular_block_rank) * 2 ** 20
    random_jitter = jax.random.randint(k_score, (N_DP, SEGS, N_MEM), 0, 2 ** 21)
    retrieval_score = (random_jitter + score_boost_extra[:, None, :]) * N_MEM + jnp.arange(N_MEM)[None, None, :]
    chosen = lax.top_k(retrieval_score, 5)[1].astype(jnp.int32)
    first = jax.random.randint(k_first, (N_DP, SEGS, 5), 0, MB_DEV)
    second = (first + jax.random.randint(k_step, (N_DP, SEGS, 5), 1, MB_DEV)) % MB_DEV
    base_id = chosen * MB_DEV
    listed = jnp.concatenate([base_id + first, (base_id + second)[:, :, :3]], axis=-1)
    shuffle = jax.random.randint(k_order, (N_DP, SEGS, TOPB), 0, 2 ** 20) * TOPB + jnp.arange(TOPB)[None, None, :]
    order = jnp.argsort(shuffle, axis=-1)
    return jnp.take_along_axis(listed, order, axis=-1).astype(jnp.int32)


def block_levels(key, shape, shards, least, high):
    level = 1.0
    for position, shards_of in shards:
        heights = jax.random.uniform(jax.random.fold_in(jax.random.fold_in(key, 6), position), (shards_of,), jnp.float32, least / len(shards), high / len(shards))
        level = level * jnp.repeat(jnp.exp(heights), shape[position] // shards_of).reshape((-1,) + (1,) * (len(shape) - 1 - position))
    return level


def noise(stream_key, extent, scale, most, cuts=(), held_as=jnp.bfloat16):
    entries = jax.random.normal(stream_key, extent, jnp.float32) * scale
    if len(cuts) > 0:
        entries = block_levels(stream_key, extent, cuts, -0.22, 0.18) * entries
    return jnp.clip(entries, min=-most, max=most).astype(held_as)


def setup_inputs(seed: int = 0) -> dict:
    arg_keys = jax.random.split(jax.random.key(seed), 7)
    tokens = draw_tokens(jax.random.fold_in(arg_keys[6], 71), 0)
    q_weight = draw_q_weight(jax.random.fold_in(arg_keys[6], 71), 0)
    memory_keys = draw_memory_keys(jax.random.fold_in(arg_keys[6], 71), 0)
    memory_values = noise(arg_keys[3], (N_DP, BLOCKS, BLOCK, KVW), 1.0, 6.0, ((0, 16), (1, 16)))
    retrieved_block_index = draw_retrieved_block_index(jax.random.fold_in(arg_keys[6], 71), 0)
    d_context = noise(arg_keys[5], (ROWS, QW), 1.0, 6.0, ((0, 256),))
    return dict(tokens=tokens, q_weight=q_weight, memory_keys=memory_keys, memory_values=memory_values, retrieved_block_index=retrieved_block_index, d_context=d_context)


def reference(tokens, q_weight, memory_keys, memory_values, retrieved_block_index, d_context):
    score_scale = 1.0 / (HD ** 0.5)
    queries = jnp.dot(tokens, q_weight, preferred_element_type=jnp.float32).astype(jnp.bfloat16)
    count_segments = ROWS // SEG
    query_blocks = queries.reshape(count_segments, SEG, QW)
    grad_blocks = d_context.reshape(count_segments, SEG, QW)
    id_lists = retrieved_block_index.reshape(count_segments, TOPB).astype(jnp.int32)
    group_index = (jnp.arange(count_segments) // N_MEM).astype(jnp.int32)

    def segment_step(items):
        seg_query, seg_grad, desired_blocks, group_id = items
        keys = memory_keys[group_id][desired_blocks].reshape(TOPB * BLOCK, KVH, HD).astype(jnp.float32)
        values = memory_values[group_id][desired_blocks].reshape(TOPB * BLOCK, KVH, HD).astype(jnp.float32)
        heads = seg_query.reshape(SEG, KVH, GRP, HD).astype(jnp.float32)
        scores = jnp.einsum('skrd,tkd->krst', heads, keys) * score_scale
        top = jnp.max(scores, axis=-1, keepdims=True)
        expo = jnp.exp(scores - top)
        probs = expo / jnp.sum(expo, axis=-1, keepdims=True)
        probs_low = probs.astype(jnp.bfloat16).astype(jnp.float32)
        context = jnp.einsum('krst,tkd->skrd', probs_low, values).reshape(SEG, QW).astype(jnp.bfloat16)
        d_out = seg_grad.reshape(SEG, KVH, GRP, HD).astype(jnp.float32)
        d_probs = jnp.einsum('skrd,tkd->krst', d_out, values)
        row_delta = jnp.sum(probs * d_probs, axis=-1, keepdims=True)
        d_scores = (probs * (d_probs - row_delta) * score_scale).astype(jnp.bfloat16).astype(jnp.float32)
        d_query = jnp.einsum('krst,tkd->skrd', d_scores, keys).reshape(SEG, QW).astype(jnp.bfloat16)
        return context, d_query

    context, d_query = lax.map(segment_step, (query_blocks, grad_blocks, id_lists, group_index))
    context = context.reshape(ROWS, QW)
    d_query = d_query.reshape(ROWS, QW)
    grad_tokens = jnp.dot(d_query, q_weight.T, preferred_element_type=jnp.float32).astype(jnp.bfloat16)
    grad_q_weight = jnp.dot(tokens.T, d_query, preferred_element_type=jnp.float32)
    return context, grad_tokens, grad_q_weight
```

```python
import math

import jax
import jax.numpy as jnp
from jax import lax
from jax.experimental import pallas as pl
from jax.experimental.pallas import tpu as pltpu
from jax.sharding import PartitionSpec as P

KVH = 4
HD = 128
TOPB = 8
SEG = 512
D = 2048
QW = 1024
NZ = 8
NMEM = 16
NDP = 16
BLK = 4
ROWS = 256
SCALE = 1.0 / HD**0.5
EXP2_SCALE = SCALE * math.log2(math.e)
MESH = pl.DeviceIdType.MESH
F32 = jnp.float32
BF16 = jnp.bfloat16


def dot(a, b):
    return jnp.dot(a, b, preferred_element_type=F32)


def kernel(
    tok_hbm, qw_hbm, mk_hbm, mv_hbm, idx, dctx_hbm,
    ctx_hbm, gt_hbm, gw_hbm,
    kv0, kv1, kv2, kv3, tok, qw, dctx, tok_t, qw_t, q, ctx, dq, gt,
    k_sel, k_t, v_one, v_t,
    g_keep, g_send, g_recv, g_sum, dp_recv,
    za_send, za_recv, zb_send, zb_recv, gw,
    in_sem, own_sem, ring_send, ring_recv, sib_send, sib_recv,
    pair_send, pair_recv, dp_send, dp_rsem, z_send, z_rsem, out_sem,
):
    kv = (kv0, kv1, kv2, kv3)
    dp = lax.axis_index("dp")
    mem = lax.axis_index("mem")
    z = lax.div(mem, 2)
    core = lax.rem(mem, 2)

    def at_z(step):
        return lax.rem(z + step + NZ, NZ) * 2 + core

    def dev(m):
        return (dp, m)

    sib = dev(z * 2 + 1 - core)

    def shard(m):
        return pl.ds(pl.multiple_of(m * BLK, BLK), BLK)

    loads = [
        pltpu.make_async_copy(tok_hbm, tok, in_sem.at[0]),
        pltpu.make_async_copy(qw_hbm, qw, in_sem.at[1]),
        pltpu.make_async_copy(dctx_hbm, dctx, in_sem.at[2]),
    ]
    own = [
        [
            pltpu.make_async_copy(
                src.at[0, :, :, pl.ds(h * HD, HD)], kv[h].at[t, shard(mem)], own_sem.at[h, t]
            )
            for t, src in enumerate((mk_hbm, mv_hbm))
        ]
        for h in range(KVH)
    ]
    for h in range(KVH):
        for c in own[h]:
            c.start()
    for c in loads:
        c.start()

    barrier = pltpu.get_barrier_semaphore()

    def greet(j, carry):
        pl.semaphore_signal(
            barrier, inc=1, device_id=dev(lax.rem(mem + j, NMEM)), device_id_type=MESH
        )
        pl.semaphore_signal(
            barrier, inc=1, device_id=(lax.rem(dp + j, NDP), mem), device_id_type=MESH
        )
        return carry

    lax.fori_loop(1, NMEM, greet, 0)
    pl.semaphore_wait(barrier, 2 * (NMEM - 1))

    def ring(h, t, way, step):
        sign = 1 if way == 0 else -1
        piece = kv[h].at[t, shard(at_z(-sign * (step - 1)))]
        return pltpu.make_async_remote_copy(
            src_ref=piece, dst_ref=piece,
            send_sem=ring_send.at[h, t], recv_sem=ring_recv.at[h, t, way, step - 1],
            device_id=dev(at_z(sign)), device_id_type=MESH,
        )

    def ring_arrival(h, t, way, step):
        sign = 1 if way == 0 else -1
        piece = kv[h].at[t, shard(at_z(-sign * step))]
        pltpu.make_async_remote_copy(
            src_ref=piece, dst_ref=piece,
            send_sem=ring_send.at[h, t], recv_sem=ring_recv.at[h, t, way, step - 1],
            device_id=dev(at_z(sign)), device_id_type=MESH,
        ).wait_recv()

    def to_sib(h, m):
        piece = kv[h].at[:, shard(m)]
        pltpu.make_async_remote_copy(
            src_ref=piece, dst_ref=piece, send_sem=sib_send.at[h], recv_sem=sib_recv.at[h],
            device_id=sib, device_id_type=MESH,
        ).start()

    def sib_all(h):
        half = kv[h].at[:, pl.ds(0, NZ * BLK)]
        return pltpu.make_async_remote_copy(
            src_ref=half, dst_ref=half, send_sem=sib_send.at[h], recv_sem=sib_recv.at[h],
            device_id=sib, device_id_type=MESH,
        )

    def send_own(h):
        for t in range(2):
            own[h][t].wait()
            for way in range(2):
                ring(h, t, way, 1).start()
        to_sib(h, mem)

    def ring_step(h, t, step):
        for way in range(2):
            if step < 4 or t == way:
                ring_arrival(h, t, way, step)
                if step < 3 or (step == 3 and t == way):
                    ring(h, t, way, step + 1).start()

    def pass_to_sib(h, step):
        to_sib(h, at_z(-step))
        if step < 4:
            to_sib(h, at_z(step))

    def gather(h):
        for j in range(TOPB):
            b = idx[0, 0, j]
            rows = pl.ds(j * 128, 128)
            kb = kv[h][0, b]
            vb = kv[h][1, b]
            k_sel[rows, :] = kb
            k_t[:, rows] = kb.T
            v_one[rows, pl.ds(0, HD)] = vb
            v_t[:, rows] = vb.T

    def attend(h, first, r):
        j = 1 - core if first else core
        rows = pl.ds(r * ROWS, ROWS)
        sub = pl.ds(pl.multiple_of(j * HD, HD), HD)
        full = pl.ds(pl.multiple_of((2 * h + j) * HD, HD), HD)
        do = dctx[rows, full]
        s = dot(q[h, rows, sub], k_t[...])
        top = jnp.max(s, axis=-1, keepdims=True)
        e = jnp.exp2((s - top) * EXP2_SCALE)
        pv = dot(e.astype(BF16), v_one[...])
        inv = 1.0 / pv[:, HD:]
        c = pv[:, :HD] * inv
        ctx[rows, full] = c.astype(BF16)
        d_p = dot(do, v_t[...])
        delta = jnp.sum(do.astype(F32) * c, axis=-1, keepdims=True)
        ds = (e * (d_p - delta)).astype(BF16)
        dq[h, rows, sub] = (dot(ds, k_sel[...]) * (inv * SCALE)).astype(BF16)

    def weight_grad(h):
        def tile(i, carry):
            rows = pl.ds(pl.multiple_of(i * 256, 256), 256)
            g = dot(tok_t[rows, :], dq[h])
            lo, hi = g[:, :HD], g[:, HD:]
            g_keep[rows, :] = jnp.where(core == 0, lo, hi)
            g_send[h, rows, :] = jnp.where(core == 0, hi, lo).astype(BF16)
            return carry

        lax.fori_loop(0, D // 256, tile, 0)
        pair(h).start()

    def pair(h):
        return pltpu.make_async_remote_copy(
            src_ref=g_send.at[h], dst_ref=g_recv.at[h], send_sem=pair_send.at[h],
            recv_sem=pair_recv.at[h], device_id=sib, device_id_type=MESH,
        )

    def dp_start(h):
        pair(h).wait_recv()

        def tile(i, carry):
            rows = pl.ds(pl.multiple_of(i * 256, 256), 256)
            g_sum[h, rows, :] = (g_keep[rows, :] + g_recv[h, rows, :].astype(F32)).astype(BF16)
            return carry

        lax.fori_loop(0, D // 256, tile, 0)

        def send(j, carry):
            d = lax.rem(dp + j, NDP)
            pltpu.make_async_remote_copy(
                src_ref=g_sum.at[h, pl.ds(pl.multiple_of(d * 128, 128), 128)],
                dst_ref=dp_recv.at[h, j - 1], send_sem=dp_send.at[h], recv_sem=dp_rsem.at[h],
                device_id=(d, mem), device_id_type=MESH,
            ).start()
            return carry

        lax.fori_loop(1, NDP, send, 0)

    def dp_all(h):
        return pltpu.make_async_remote_copy(
            src_ref=dp_recv.at[h], dst_ref=dp_recv.at[h], send_sem=dp_send.at[h],
            recv_sem=dp_rsem.at[h], device_id=sib, device_id_type=MESH,
        )

    def dp_finish(h):
        dp_all(h).wait_recv()
        acc = g_sum[h, pl.ds(pl.multiple_of(dp * 128, 128), 128), :].astype(F32)
        for j in range(NDP - 1):
            acc = acc + dp_recv[h, j].astype(F32)
        acc = acc.reshape(NMEM, 8, HD)
        if h < KVH - 1:
            za_send[:, :, pl.ds(h * HD, HD)] = acc
        else:
            zb_send[...] = acc

    def z_start(n, src, dst):
        def send(j, carry):
            m = lax.rem(mem + j, NMEM)
            pltpu.make_async_remote_copy(
                src_ref=src.at[m], dst_ref=dst.at[j - 1], send_sem=z_send.at[n],
                recv_sem=z_rsem.at[n], device_id=dev(m), device_id_type=MESH,
            ).start()
            return carry

        lax.fori_loop(1, NMEM, send, 0)

    def z_all(n, dst):
        return pltpu.make_async_remote_copy(
            src_ref=dst, dst_ref=dst, send_sem=z_send.at[n], recv_sem=z_rsem.at[n],
            device_id=sib, device_id_type=MESH,
        )

    def z_finish(n, src, dst, heads):
        z_all(n, dst).wait_recv()
        same = src[mem]
        other = dst[0]
        for j in range(2, NMEM):
            if j % 2 == 0:
                same = same + dst[j - 1]
            else:
                other = other + dst[j - 1]
        for i, h in enumerate(heads):
            part = slice(i * HD, (i + 1) * HD)
            gw[:, pl.ds(pl.multiple_of(h * 256 + core * HD, HD), HD)] = same[:, part]
            gw[:, pl.ds(pl.multiple_of(h * 256 + (1 - core) * HD, HD), HD)] = other[:, part]

    v_one[:, pl.ds(HD, HD)] = jnp.ones((TOPB * 128, HD), BF16)

    send_own(0)
    send_own(1)

    def project(n):
        if n == 0:
            loads[0].wait()
            loads[1].wait()
        q[n] = dot(tok[...], qw[:, pl.ds(n * 256, 256)]).astype(BF16)

    def transposes(n):
        tok_t[pl.ds(n * 512, 512), :] = tok[:, pl.ds(n * 512, 512)].T
        qw_t[:, pl.ds(n * 512, 512)] = qw[pl.ds(n * 512, 512), :].T

    for h in range(KVH):
        for step in range(1, 5):
            ring_step(h, 0, step)
            if h == 0:
                project(step - 1)
            elif step == 2 and h >= 2:
                dp_start(h - 2)
            elif step == 3 and h == 1:
                pass
            ring_step(h, 1, step)
            pass_to_sib(h, step)
            if step == 2 and 1 <= h < KVH - 1:
                send_own(h + 1)
            if h == 0:
                transposes(step - 1)
                if step == 4:
                    loads[2].wait()
            else:
                attend(h - 1, step <= 2, (step - 1) % 2)
        if h >= 2:
            dp_finish(h - 2)
        sib_all(h).wait_recv()
        if h >= 1:
            weight_grad(h - 1)
        gather(h)

    dp_start(2)
    for step in range(4):
        attend(3, step < 2, step % 2)
    weight_grad(3)
    dp_finish(2)
    z_start(0, za_send, za_recv)
    ctx_out = pltpu.make_async_copy(ctx, ctx_hbm, out_sem.at[0])
    ctx_out.start()
    dp_start(3)

    def tokens_tile(n, carry):
        cols = pl.ds(pl.multiple_of(n * 512, 512), 512)
        acc = dot(dq[0], qw_t[pl.ds(0, 256), cols])
        for h in range(1, KVH):
            acc = acc + dot(dq[h], qw_t[pl.ds(h * 256, 256), cols])
        gt[:, cols] = acc.astype(BF16)
        return carry

    lax.fori_loop(0, D // 512, tokens_tile, 0)
    gt_out = pltpu.make_async_copy(gt, gt_hbm, out_sem.at[1])
    gt_out.start()
    z_finish(0, za_send, za_recv, (0, 1, 2))
    dp_finish(3)
    z_start(1, zb_send, zb_recv)
    z_finish(1, zb_send, zb_recv, (3,))
    gw_out = pltpu.make_async_copy(gw, gw_hbm, out_sem.at[2])
    gw_out.start()

    for h in range(KVH):
        for t in range(2):
            sent = kv[h].at[t, pl.ds(0, 7 * BLK)]
            pltpu.make_async_remote_copy(
                src_ref=sent, dst_ref=sent, send_sem=ring_send.at[h, t],
                recv_sem=ring_recv.at[h, t, 0, 0], device_id=sib, device_id_type=MESH,
            ).wait_send()
        sib_all(h).wait_send()
        pair(h).wait_send()
        dp_all(h).wait_send()
    z_all(0, za_recv).wait_send()
    z_all(1, zb_recv).wait_send()
    ctx_out.wait()
    gt_out.wait()
    gw_out.wait()


def on_device(tokens, q_weight, memory_keys, memory_values, retrieved_block_index, d_context):
    hbm = pl.BlockSpec(memory_space=pl.ANY)
    vmem = pltpu.VMEM
    dma = pltpu.SemaphoreType.DMA
    kv = vmem((2, NMEM * BLK, 128, HD), BF16)
    return pl.pallas_call(
        kernel,
        out_shape=(
            jax.ShapeDtypeStruct((SEG, QW), BF16),
            jax.ShapeDtypeStruct((SEG, D), BF16),
            jax.ShapeDtypeStruct((D // (NDP * NMEM), QW), F32),
        ),
        in_specs=[hbm, hbm, hbm, hbm, pl.BlockSpec(memory_space=pltpu.SMEM), hbm],
        out_specs=(hbm, hbm, hbm),
        scratch_shapes=[
            kv, kv, kv, kv,
            vmem((SEG, D), BF16),
            vmem((D, QW), BF16),
            vmem((SEG, QW), BF16),
            vmem((D, SEG), BF16),
            vmem((QW, D), BF16),
            vmem((KVH, SEG, 256), BF16),
            vmem((SEG, QW), BF16),
            vmem((KVH, SEG, 256), BF16),
            vmem((SEG, D), BF16),
            vmem((TOPB * 128, HD), BF16),
            vmem((HD, TOPB * 128), BF16),
            vmem((TOPB * 128, 2 * HD), BF16),
            vmem((HD, TOPB * 128), BF16),
            vmem((D, HD), F32),
            vmem((KVH, D, HD), BF16),
            vmem((KVH, D, HD), BF16),
            vmem((KVH, D, HD), BF16),
            vmem((KVH, NDP - 1, 128, HD), BF16),
            vmem((NMEM, 8, 3 * HD), F32),
            vmem((NMEM - 1, 8, 3 * HD), F32),
            vmem((NMEM, 8, HD), F32),
            vmem((NMEM - 1, 8, HD), F32),
            vmem((8, QW), F32),
            dma((3,)),
            dma((KVH, 2)),
            dma((KVH, 2)),
            dma((KVH, 2, 2, 4)),
            dma((KVH,)),
            dma((KVH,)),
            dma((KVH,)),
            dma((KVH,)),
            dma((KVH,)),
            dma((KVH,)),
            dma((2,)),
            dma((2,)),
            dma((3,)),
        ],
        compiler_params=pltpu.CompilerParams(
            collective_id=0, has_side_effects=True, vmem_limit_bytes=60 * 1024 * 1024
        ),
    )(tokens, q_weight, memory_keys, memory_values, retrieved_block_index, d_context)


def solution(mesh):
    return jax.shard_map(
        on_device,
        mesh=mesh,
        in_specs=(
            P(("dp", "mem"), None),
            P(),
            P("dp", "mem", None, None),
            P("dp", "mem", None, None),
            P("dp", "mem", None),
            P(("dp", "mem"), None),
        ),
        out_specs=(P(("dp", "mem"), None), P(("dp", "mem"), None), P(("dp", "mem"), None)),
        check_vma=False,
    )
```

```python
import math

import jax
import jax.numpy as jnp
from jax import lax
from jax.experimental import pallas as pl
from jax.experimental.pallas import tpu as pltpu
from jax.sharding import PartitionSpec as P

KVH = 4
HD = 128
TOPB = 8
SEG = 512
D = 2048
QW = 1024
NZ = 8
NMEM = 16
NDP = 16
BLK = 4
ROWS = 256
SCALE = 1.0 / HD**0.5
EXP2_SCALE = SCALE * math.log2(math.e)
MESH = pl.DeviceIdType.MESH
F32 = jnp.float32
BF16 = jnp.bfloat16


def dot(a, b):
    return jnp.dot(a, b, preferred_element_type=F32)


def kernel(
    tok_hbm, qw_hbm, mk_hbm, mv_hbm, idx, dctx_hbm,
    ctx, gt, gw,
    kv0, kv1, kv2, kv3, tok, qw, dctx, tok_t, qw_t, q, dq,
    k_sel, k_t, v_one, v_t,
    g_keep, g_send, g_recv, g_sum, dp_recv,
    za_send, za_recv, zb_send, zb_recv,
    in_sem, own_sem, ring_send, ring_recv, sib_send, sib_recv,
    pair_send, pair_recv, dp_send, dp_rsem, z_send, z_rsem,
):
    kv = (kv0, kv1, kv2, kv3)
    dp = lax.axis_index("dp")
    mem = lax.axis_index("mem")
    z = lax.div(mem, 2)
    core = lax.rem(mem, 2)

    def at_z(step):
        return lax.rem(z + step + NZ, NZ) * 2 + core

    def dev(m):
        return (dp, m)

    sib = dev(z * 2 + 1 - core)

    def shard(m):
        return pl.ds(pl.multiple_of(m * BLK, BLK), BLK)

    loads = [
        pltpu.make_async_copy(tok_hbm, tok, in_sem.at[0]),
        pltpu.make_async_copy(qw_hbm, qw, in_sem.at[1]),
        pltpu.make_async_copy(dctx_hbm, dctx, in_sem.at[2]),
    ]
    own = [
        [
            pltpu.make_async_copy(
                src.at[0, :, :, pl.ds(h * HD, HD)], kv[h].at[t, shard(mem)], own_sem.at[h, t]
            )
            for t, src in enumerate((mk_hbm, mv_hbm))
        ]
        for h in range(KVH)
    ]
    for h in range(KVH):
        for c in own[h]:
            c.start()
    for c in loads:
        c.start()

    barrier = pltpu.get_barrier_semaphore()

    def greet(j, carry):
        pl.semaphore_signal(
            barrier, inc=1, device_id=dev(lax.rem(mem + j, NMEM)), device_id_type=MESH
        )
        pl.semaphore_signal(
            barrier, inc=1, device_id=(lax.rem(dp + j, NDP), mem), device_id_type=MESH
        )
        return carry

    lax.fori_loop(1, NMEM, greet, 0)
    pl.semaphore_wait(barrier, 2 * (NMEM - 1))

    def ring(h, t, way, step):
        sign = 1 if way == 0 else -1
        piece = kv[h].at[t, shard(at_z(-sign * (step - 1)))]
        return pltpu.make_async_remote_copy(
            src_ref=piece, dst_ref=piece,
            send_sem=ring_send.at[h, t], recv_sem=ring_recv.at[h, t, way, step - 1],
            device_id=dev(at_z(sign)), device_id_type=MESH,
        )

    def ring_arrival(h, t, way, step):
        sign = 1 if way == 0 else -1
        piece = kv[h].at[t, shard(at_z(-sign * step))]
        pltpu.make_async_remote_copy(
            src_ref=piece, dst_ref=piece,
            send_sem=ring_send.at[h, t], recv_sem=ring_recv.at[h, t, way, step - 1],
            device_id=dev(at_z(sign)), device_id_type=MESH,
        ).wait_recv()

    def to_sib(h, m):
        piece = kv[h].at[:, shard(m)]
        pltpu.make_async_remote_copy(
            src_ref=piece, dst_ref=piece, send_sem=sib_send.at[h], recv_sem=sib_recv.at[h],
            device_id=sib, device_id_type=MESH,
        ).start()

    def sib_all(h):
        half = kv[h].at[:, pl.ds(0, NZ * BLK)]
        return pltpu.make_async_remote_copy(
            src_ref=half, dst_ref=half, send_sem=sib_send.at[h], recv_sem=sib_recv.at[h],
            device_id=sib, device_id_type=MESH,
        )

    def send_own(h):
        for t in range(2):
            own[h][t].wait()
            for way in range(2):
                ring(h, t, way, 1).start()
        to_sib(h, mem)

    def ring_step(h, step):
        for t in range(2):
            for way in range(2):
                if step < 4 or t == way:
                    ring_arrival(h, t, way, step)
                    if step < 3 or (step == 3 and t == way):
                        ring(h, t, way, step + 1).start()
        to_sib(h, at_z(-step))
        if step < 4:
            to_sib(h, at_z(step))

    def gather(h):
        for j in range(TOPB):
            b = idx[0, 0, j]
            rows = pl.ds(j * 128, 128)
            kb = kv[h][0, b]
            vb = kv[h][1, b]
            k_sel[rows, :] = kb
            k_t[:, rows] = kb.T
            v_one[rows, pl.ds(0, HD)] = vb
            v_t[:, rows] = vb.T

    def attend(h, first, r):
        j = 1 - core if first else core
        rows = pl.ds(r * ROWS, ROWS)
        sub = pl.ds(pl.multiple_of(j * HD, HD), HD)
        full = pl.ds(pl.multiple_of((2 * h + j) * HD, HD), HD)
        do = dctx[rows, full]
        s = dot(q[h, rows, sub], k_t[...])
        top = jnp.max(s, axis=-1, keepdims=True)
        e = jnp.exp2((s - top) * EXP2_SCALE)
        pv = dot(e.astype(BF16), v_one[...])
        inv = 1.0 / pv[:, HD:]
        c = pv[:, :HD] * inv
        ctx[rows, full] = c.astype(BF16)
        d_p = dot(do, v_t[...])
        delta = jnp.sum(do.astype(F32) * c, axis=-1, keepdims=True)
        ds = (e * (d_p - delta)).astype(BF16)
        dq[h, rows, sub] = (dot(ds, k_sel[...]) * (inv * SCALE)).astype(BF16)

    def weight_grad(h, first):
        j = 1 - core if first else core
        sub = pl.ds(pl.multiple_of(j * HD, HD), HD)

        def tile(i, carry):
            rows = pl.ds(pl.multiple_of(i * 1024, 1024), 1024)
            g = dot(tok_t[rows, :], dq[h, :, sub])
            if first:
                g_send[h, rows, :] = g.astype(BF16)
            else:
                g_keep[rows, :] = g
            return carry

        lax.fori_loop(0, D // 1024, tile, 0)
        if first:
            pair(h).start()

    def pair(h):
        return pltpu.make_async_remote_copy(
            src_ref=g_send.at[h], dst_ref=g_recv.at[h], send_sem=pair_send.at[h],
            recv_sem=pair_recv.at[h], device_id=sib, device_id_type=MESH,
        )

    def dp_start(h):
        pair(h).wait_recv()

        def tile(i, carry):
            rows = pl.ds(pl.multiple_of(i * 256, 256), 256)
            g_sum[h, rows, :] = (g_keep[rows, :] + g_recv[h, rows, :].astype(F32)).astype(BF16)
            return carry

        lax.fori_loop(0, D // 256, tile, 0)

        def send(j, carry):
            d = lax.rem(dp + j, NDP)
            pltpu.make_async_remote_copy(
                src_ref=g_sum.at[h, pl.ds(pl.multiple_of(d * 128, 128), 128)],
                dst_ref=dp_recv.at[h, j - 1], send_sem=dp_send.at[h], recv_sem=dp_rsem.at[h],
                device_id=(d, mem), device_id_type=MESH,
            ).start()
            return carry

        lax.fori_loop(1, NDP, send, 0)

    def dp_all(h):
        return pltpu.make_async_remote_copy(
            src_ref=dp_recv.at[h], dst_ref=dp_recv.at[h], send_sem=dp_send.at[h],
            recv_sem=dp_rsem.at[h], device_id=sib, device_id_type=MESH,
        )

    def dp_finish(h):
        dp_all(h).wait_recv()
        acc = g_sum[h, pl.ds(pl.multiple_of(dp * 128, 128), 128), :].astype(F32)
        for j in range(NDP - 1):
            acc = acc + dp_recv[h, j].astype(F32)
        acc = acc.reshape(NMEM, 8, HD)
        if h < KVH - 1:
            za_send[:, :, pl.ds(h * HD, HD)] = acc
        else:
            zb_send[...] = acc

    def z_start(n, src, dst):
        def send(j, carry):
            m = lax.rem(mem + j, NMEM)
            pltpu.make_async_remote_copy(
                src_ref=src.at[m], dst_ref=dst.at[j - 1], send_sem=z_send.at[n],
                recv_sem=z_rsem.at[n], device_id=dev(m), device_id_type=MESH,
            ).start()
            return carry

        lax.fori_loop(1, NMEM, send, 0)

    def z_all(n, dst):
        return pltpu.make_async_remote_copy(
            src_ref=dst, dst_ref=dst, send_sem=z_send.at[n], recv_sem=z_rsem.at[n],
            device_id=sib, device_id_type=MESH,
        )

    def z_finish(n, src, dst, heads):
        z_all(n, dst).wait_recv()
        same = src[mem]
        other = dst[0]
        for j in range(2, NMEM):
            if j % 2 == 0:
                same = same + dst[j - 1]
            else:
                other = other + dst[j - 1]
        for i, h in enumerate(heads):
            part = slice(i * HD, (i + 1) * HD)
            gw[:, pl.ds(pl.multiple_of(h * 256 + core * HD, HD), HD)] = same[:, part]
            gw[:, pl.ds(pl.multiple_of(h * 256 + (1 - core) * HD, HD), HD)] = other[:, part]

    v_one[:, pl.ds(HD, HD)] = jnp.ones((TOPB * 128, HD), BF16)

    send_own(0)
    send_own(1)

    def project(n):
        if n == 0:
            loads[0].wait()
            loads[1].wait()
        q[n] = dot(tok[...], qw[:, pl.ds(n * 256, 256)]).astype(BF16)

    def transposes(n):
        tok_t[pl.ds(n * 512, 512), :] = tok[:, pl.ds(n * 512, 512)].T
        qw_t[:, pl.ds(n * 512, 512)] = qw[pl.ds(n * 512, 512), :].T

    def prepare(h):
        sib_all(h).wait_recv()
        gather(h)

    def part(h, n):
        attend(h, n < 2, n % 2)
        if n % 2 == 1:
            weight_grad(h, n < 2)

    ring_step(0, 1)
    project(0)
    project(1)
    ring_step(0, 2)
    project(2)
    ring_step(1, 1)
    project(3)
    transposes(0)
    ring_step(0, 3)
    transposes(1)
    send_own(2)
    ring_step(0, 4)
    transposes(2)
    ring_step(1, 2)
    transposes(3)
    loads[2].wait()
    prepare(0)
    part(0, 0)
    ring_step(2, 1)
    part(0, 1)
    ring_step(1, 3)
    part(0, 2)
    send_own(3)
    ring_step(1, 4)
    part(0, 3)
    ring_step(2, 2)
    prepare(1)
    part(1, 0)
    dp_start(0)
    ring_step(3, 1)
    part(1, 1)
    ring_step(2, 3)
    part(1, 2)
    ring_step(2, 4)
    part(1, 3)
    ring_step(3, 2)
    prepare(2)
    part(2, 0)
    dp_start(1)
    ring_step(3, 3)
    part(2, 1)
    part(2, 2)
    part(2, 3)
    dp_finish(0)
    ring_step(3, 4)
    dp_start(2)
    prepare(3)
    part(3, 0)
    part(3, 1)
    part(3, 2)
    part(3, 3)
    dp_start(3)
    dp_finish(1)
    dp_finish(2)
    z_start(0, za_send, za_recv)

    def tokens_tile(n, carry):
        cols = pl.ds(pl.multiple_of(n * 512, 512), 512)
        acc = dot(dq[0], qw_t[pl.ds(0, 256), cols])
        for h in range(1, KVH):
            acc = acc + dot(dq[h], qw_t[pl.ds(h * 256, 256), cols])
        gt[:, cols] = acc.astype(BF16)
        return carry

    lax.fori_loop(0, D // 512, tokens_tile, 0)
    z_finish(0, za_send, za_recv, (0, 1, 2))
    dp_finish(3)
    z_start(1, zb_send, zb_recv)
    z_finish(1, zb_send, zb_recv, (3,))

    for h in range(KVH):
        for t in range(2):
            sent = kv[h].at[t, pl.ds(0, 7 * BLK)]
            pltpu.make_async_remote_copy(
                src_ref=sent, dst_ref=sent, send_sem=ring_send.at[h, t],
                recv_sem=ring_recv.at[h, t, 0, 0], device_id=sib, device_id_type=MESH,
            ).wait_send()
        sib_all(h).wait_send()
        pair(h).wait_send()
        dp_all(h).wait_send()
    z_all(0, za_recv).wait_send()
    z_all(1, zb_recv).wait_send()


def on_device(tokens, q_weight, memory_keys, memory_values, retrieved_block_index, d_context):
    hbm = pl.BlockSpec(memory_space=pl.ANY)
    vmem = pltpu.VMEM
    dma = pltpu.SemaphoreType.DMA
    kv = vmem((2, NMEM * BLK, 128, HD), BF16)
    return pl.pallas_call(
        kernel,
        out_shape=(
            vmem((SEG, QW), BF16),
            vmem((SEG, D), BF16),
            vmem((D // (NDP * NMEM), QW), F32),
        ),
        in_specs=[hbm, hbm, hbm, hbm, pl.BlockSpec(memory_space=pltpu.SMEM), hbm],
        out_specs=(pl.BlockSpec(memory_space=vmem),) * 3,
        scratch_shapes=[
            kv, kv, kv, kv,
            vmem((SEG, D), BF16),
            vmem((D, QW), BF16),
            vmem((SEG, QW), BF16),
            vmem((D, SEG), BF16),
            vmem((QW, D), BF16),
            vmem((KVH, SEG, 256), BF16),
            vmem((KVH, SEG, 256), BF16),
            vmem((TOPB * 128, HD), BF16),
            vmem((HD, TOPB * 128), BF16),
            vmem((TOPB * 128, 2 * HD), BF16),
            vmem((HD, TOPB * 128), BF16),
            vmem((D, HD), F32),
            vmem((KVH, D, HD), BF16),
            vmem((KVH, D, HD), BF16),
            vmem((KVH, D, HD), BF16),
            vmem((KVH, NDP - 1, 128, HD), BF16),
            vmem((NMEM, 8, 3 * HD), F32),
            vmem((NMEM - 1, 8, 3 * HD), F32),
            vmem((NMEM, 8, HD), F32),
            vmem((NMEM - 1, 8, HD), F32),
            dma((3,)),
            dma((KVH, 2)),
            dma((KVH, 2)),
            dma((KVH, 2, 2, 4)),
            dma((KVH,)),
            dma((KVH,)),
            dma((KVH,)),
            dma((KVH,)),
            dma((KVH,)),
            dma((KVH,)),
            dma((2,)),
            dma((2,)),
        ],
        compiler_params=pltpu.CompilerParams(
            collective_id=0, has_side_effects=True, vmem_limit_bytes=52 * 1024 * 1024
        ),
    )(tokens, q_weight, memory_keys, memory_values, retrieved_block_index, d_context)


def solution(mesh):
    return jax.shard_map(
        on_device,
        mesh=mesh,
        in_specs=(
            P(("dp", "mem"), None),
            P(),
            P("dp", "mem", None, None),
            P("dp", "mem", None, None),
            P("dp", "mem", None),
            P(("dp", "mem"), None),
        ),
        out_specs=(P(("dp", "mem"), None), P(("dp", "mem"), None), P(("dp", "mem"), None)),
        check_vma=False,
    )
```

```python
import functools
import math
import types

import jax
import jax.numpy as jnp
from jax import lax
from jax.experimental import pallas as pl
from jax.experimental.pallas import tpu as pltpu
from jax.sharding import PartitionSpec as P

KVH = 4
HD = 128
TOPB = 8
SEG = 512
D = 2048
QW = 1024
NZ = 8
NMEM = 16
NDP = 16
BLK = 4
CHIP = 2 * BLK
ROWS = 256
ROUNDS = 9
WIDE = 2
LAG = 2
SLOTS = ROUNDS * WIDE
SCALE = 1.0 / HD**0.5
EXP2_SCALE = SCALE * math.log2(math.e)
MESH = pl.DeviceIdType.MESH
F32 = jnp.float32
BF16 = jnp.bfloat16
I32 = jnp.int32


def dot(a, b):
    return jnp.dot(a, b, preferred_element_type=F32)


def scratch(wanted):
    vmem, dma = pltpu.VMEM, pltpu.SemaphoreType.DMA
    table = dict(
        tok=vmem((SEG, D), BF16),
        qw=vmem((D, QW), BF16),
        dctx=vmem((SEG, QW), BF16),
        tok_t=vmem((D, SEG), BF16),
        qw_t=vmem((QW, D), BF16),
        q=vmem((KVH, SEG, 256), BF16),
        dq=vmem((KVH, SEG, 256), BF16),
        k_sel=vmem((TOPB * 128, HD), BF16),
        k_t=vmem((HD, TOPB * 128), BF16),
        v_one=vmem((TOPB * 128, 2 * HD), BF16),
        v_t=vmem((HD, TOPB * 128), BF16),
        g_keep=vmem((D, HD), F32),
        g_send=vmem((KVH, D, HD), BF16),
        g_recv=vmem((KVH, D, HD), BF16),
        g_sum=vmem((KVH, D, HD), BF16),
        dp_recv=vmem((KVH, NDP - 1, 128, HD), BF16),
        za_send=vmem((NMEM, 8, 3 * HD), F32),
        za_recv=vmem((NMEM - 1, 8, 3 * HD), F32),
        zb_send=vmem((NMEM, 8, HD), F32),
        zb_recv=vmem((NMEM - 1, 8, HD), F32),
        in_sem=dma((3,)),
        own_sem=dma((KVH, 2)),
        sib_send=dma((KVH,)),
        sib_recv=dma((KVH,)),
        pair_send=dma((KVH,)),
        pair_recv=dma((KVH,)),
        dp_send=dma((KVH,)),
        dp_rsem=dma((KVH,)),
        z_send=dma((2,)),
        z_rsem=dma((2,)),
    )
    table.update(wanted)
    return table


def slow_scratch():
    vmem, dma = pltpu.VMEM, pltpu.SemaphoreType.DMA
    wanted = {"kv%d" % h: vmem((2, NMEM * BLK, 128, HD), BF16) for h in range(KVH)}
    wanted.update(ring_send=dma((KVH, 2)), ring_recv=dma((KVH, 2, 2, 4)))
    return scratch(wanted)


def fast_scratch():
    vmem, dma = pltpu.VMEM, pltpu.SemaphoreType.DMA
    wanted = {}
    for h in range(KVH):
        wanted["pool%d" % h] = vmem((CHIP + SLOTS, 2, 128, HD), BF16)
        wanted["oth%d" % h] = vmem((SLOTS, 2, 128, HD), BF16)
        wanted["rcv%d" % h] = vmem((ROUNDS, WIDE, 2, 128, HD), BF16)
        wanted["stg%d" % h] = vmem((ROUNDS, WIDE, 2, 128, HD), BF16)
    wanted.update(
        idx_own=vmem((8, 128), I32),
        idx_all=vmem((NMEM, 8, 128), I32),
        work=vmem((8, 128), I32),
        tab=pltpu.SMEM((8, 128), I32),
        flag_own=vmem((8, 128), I32),
        flag_all=vmem((NDP - 1, 8, 128), I32),
        chip_send=dma((KVH,)),
        chip_recv=dma((KVH,)),
        hop_send=dma((KVH,)),
        hop_recv=dma((KVH, ROUNDS)),
        misc=dma((5,)),
    )
    return scratch(wanted)


def kernel(fast, *refs):
    tok_hbm, qw_hbm, mk_hbm, mv_hbm, idx, dctx_hbm = refs[:6]
    n_out = 4 if fast else 3
    ctx, gt, gw = refs[6:9]
    names = fast_scratch() if fast else slow_scratch()
    v = types.SimpleNamespace(**dict(zip(names, refs[6 + n_out:])))
    dp = lax.axis_index("dp")
    mem = lax.axis_index("mem")
    z = lax.div(mem, 2)
    core = lax.rem(mem, 2)

    def at_z(step):
        return lax.rem(z + step + NZ, NZ) * 2 + core

    def dev(m):
        return (dp, m)

    sib = dev(z * 2 + 1 - core)

    def shard(m):
        return pl.ds(pl.multiple_of(m * BLK, BLK), BLK)

    def remote(src, dst, send_sem, recv_sem, device):
        return pltpu.make_async_remote_copy(
            src_ref=src, dst_ref=dst, send_sem=send_sem, recv_sem=recv_sem,
            device_id=device, device_id_type=MESH,
        )

    def whole(ref, send_sem, recv_sem):
        return remote(ref, ref, send_sem, recv_sem, sib)

    def mem_peers(send):
        def body(j, carry):
            send(j, lax.rem(mem + j, NMEM))
            return carry

        lax.fori_loop(1, NMEM, body, 0)

    def dp_peers(send):
        def body(j, carry):
            send(j, lax.rem(dp + j, NDP))
            return carry

        lax.fori_loop(1, NDP, body, 0)

    if fast:
        pool = (v.pool0, v.pool1, v.pool2, v.pool3)
        oth = (v.oth0, v.oth1, v.oth2, v.oth3)
        rcv = (v.rcv0, v.rcv1, v.rcv2, v.rcv3)
        stg = (v.stg0, v.stg1, v.stg2, v.stg3)
        mine = pl.ds(pl.multiple_of(core * BLK, BLK), BLK)
        own_place = [[pool[h].at[mine, t] for t in range(2)] for h in range(KVH)]
    else:
        kv = (v.kv0, v.kv1, v.kv2, v.kv3)
        own_place = [[kv[h].at[t, shard(mem)] for t in range(2)] for h in range(KVH)]

    loads = [
        pltpu.make_async_copy(tok_hbm, v.tok, v.in_sem.at[0]),
        pltpu.make_async_copy(qw_hbm, v.qw, v.in_sem.at[1]),
        pltpu.make_async_copy(dctx_hbm, v.dctx, v.in_sem.at[2]),
    ]
    own = [
        [
            pltpu.make_async_copy(
                src.at[0, :, :, pl.ds(h * HD, HD)], own_place[h][t], v.own_sem.at[h, t]
            )
            for t, src in enumerate((mk_hbm, mv_hbm))
        ]
        for h in range(KVH)
    ]
    for h in range(KVH):
        for c in own[h]:
            c.start()
    for c in loads:
        c.start()

    barrier = pltpu.get_barrier_semaphore()

    def greet(j, carry):
        pl.semaphore_signal(
            barrier, inc=1, device_id=dev(lax.rem(mem + j, NMEM)), device_id_type=MESH
        )
        pl.semaphore_signal(
            barrier, inc=1, device_id=(lax.rem(dp + j, NDP), mem), device_id_type=MESH
        )
        return carry

    lax.fori_loop(1, NMEM, greet, 0)
    if fast:
        for j in range(TOPB):
            v.idx_own[pl.ds(j, 1), :] = jnp.full((1, 128), idx[0, 0, j], I32)
    pl.semaphore_wait(barrier, 2 * (NMEM - 1))

    def project(n):
        if n == 0:
            loads[0].wait()
            loads[1].wait()
        v.q[n] = dot(v.tok[...], v.qw[:, pl.ds(n * 256, 256)]).astype(BF16)

    def transposes(n):
        v.tok_t[pl.ds(n * 512, 512), :] = v.tok[:, pl.ds(n * 512, 512)].T
        v.qw_t[:, pl.ds(n * 512, 512)] = v.qw[pl.ds(n * 512, 512), :].T

    def ready():
        loads[2].wait()
        v.v_one[:, pl.ds(HD, HD)] = jnp.ones((TOPB * 128, HD), BF16)

    def place(j, kb, vb):
        rows = pl.ds(j * 128, 128)
        v.k_sel[rows, :] = kb
        v.k_t[:, rows] = kb.T
        v.v_one[rows, pl.ds(0, HD)] = vb
        v.v_t[:, rows] = vb.T

    def attend(h, first, r):
        j = 1 - core if first else core
        rows = pl.ds(r * ROWS, ROWS)
        sub = pl.ds(pl.multiple_of(j * HD, HD), HD)
        full = pl.ds(pl.multiple_of((2 * h + j) * HD, HD), HD)
        do = v.dctx[rows, full]
        s = dot(v.q[h, rows, sub], v.k_t[...])
        top = jnp.max(s, axis=-1, keepdims=True)
        e = jnp.exp2((s - top) * EXP2_SCALE)
        pv = dot(e.astype(BF16), v.v_one[...])
        inv = 1.0 / pv[:, HD:]
        c = pv[:, :HD] * inv
        ctx[rows, full] = c.astype(BF16)
        d_p = dot(do, v.v_t[...])
        delta = jnp.sum(do.astype(F32) * c, axis=-1, keepdims=True)
        ds = (e * (d_p - delta)).astype(BF16)
        v.dq[h, rows, sub] = (dot(ds, v.k_sel[...]) * (inv * SCALE)).astype(BF16)

    def weight_grad(h, first):
        j = 1 - core if first else core
        sub = pl.ds(pl.multiple_of(j * HD, HD), HD)

        def tile(i, carry):
            rows = pl.ds(pl.multiple_of(i * 1024, 1024), 1024)
            g = dot(v.tok_t[rows, :], v.dq[h, :, sub])
            if first:
                v.g_send[h, rows, :] = g.astype(BF16)
            else:
                v.g_keep[rows, :] = g
            return carry

        lax.fori_loop(0, D // 1024, tile, 0)
        if first:
            pair(h).start()

    def part(h, n):
        attend(h, n < 2, n % 2)
        if n % 2 == 1:
            weight_grad(h, n < 2)

    def pair(h):
        return remote(v.g_send.at[h], v.g_recv.at[h], v.pair_send.at[h], v.pair_recv.at[h], sib)

    def dp_start(h):
        pair(h).wait_recv()

        def tile(i, carry):
            rows = pl.ds(pl.multiple_of(i * 256, 256), 256)
            total = v.g_keep[rows, :] + v.g_recv[h, rows, :].astype(F32)
            v.g_sum[h, rows, :] = total.astype(BF16)
            return carry

        lax.fori_loop(0, D // 256, tile, 0)

        def send(j, d):
            rows = pl.ds(pl.multiple_of(d * 128, 128), 128)
            remote(
                v.g_sum.at[h, rows], v.dp_recv.at[h, j - 1], v.dp_send.at[h], v.dp_rsem.at[h],
                (d, mem),
            ).start()

        dp_peers(send)

    def dp_all(h):
        return whole(v.dp_recv.at[h], v.dp_send.at[h], v.dp_rsem.at[h])

    def dp_finish(h):
        dp_all(h).wait_recv()
        acc = v.g_sum[h, pl.ds(pl.multiple_of(dp * 128, 128), 128), :].astype(F32)
        for j in range(NDP - 1):
            acc = acc + v.dp_recv[h, j].astype(F32)
        acc = acc.reshape(NMEM, 8, HD)
        if h < KVH - 1:
            v.za_send[:, :, pl.ds(h * HD, HD)] = acc
        else:
            v.zb_send[...] = acc

    def z_start(n, src, dst):
        def send(j, m):
            remote(src.at[m], dst.at[j - 1], v.z_send.at[n], v.z_rsem.at[n], dev(m)).start()

        mem_peers(send)

    def z_all(n, dst):
        return whole(dst, v.z_send.at[n], v.z_rsem.at[n])

    def z_finish(n, src, dst, heads):
        z_all(n, dst).wait_recv()
        same = src[mem]
        other = dst[0]
        for j in range(2, NMEM):
            if j % 2 == 0:
                same = same + dst[j - 1]
            else:
                other = other + dst[j - 1]
        for i, h in enumerate(heads):
            cut = slice(i * HD, (i + 1) * HD)
            gw[:, pl.ds(pl.multiple_of(h * 256 + core * HD, HD), HD)] = same[:, cut]
            gw[:, pl.ds(pl.multiple_of(h * 256 + (1 - core) * HD, HD), HD)] = other[:, cut]

    def tail():
        dp_start(2)
        prepare(3)
        for n in range(4):
            part(3, n)
        dp_start(3)
        dp_finish(1)
        dp_finish(2)
        z_start(0, v.za_send, v.za_recv)

        def tokens_tile(n, carry):
            cols = pl.ds(pl.multiple_of(n * 512, 512), 512)
            acc = dot(v.dq[0], v.qw_t[pl.ds(0, 256), cols])
            for h in range(1, KVH):
                acc = acc + dot(v.dq[h], v.qw_t[pl.ds(h * 256, 256), cols])
            gt[:, cols] = acc.astype(BF16)
            return carry

        lax.fori_loop(0, D // 512, tokens_tile, 0)
        z_finish(0, v.za_send, v.za_recv, (0, 1, 2))
        dp_finish(3)
        z_start(1, v.zb_send, v.zb_recv)
        z_finish(1, v.zb_send, v.zb_recv, (3,))
        for h in range(KVH):
            sib_all(h).wait_send()
            pair(h).wait_send()
            dp_all(h).wait_send()
        z_all(0, v.za_recv).wait_send()
        z_all(1, v.zb_recv).wait_send()

    if not fast:
        def ring(h, t, way, step):
            sign = 1 if way == 0 else -1
            piece = kv[h].at[t, shard(at_z(-sign * (step - 1)))]
            return remote(
                piece, piece, v.ring_send.at[h, t], v.ring_recv.at[h, t, way, step - 1],
                dev(at_z(sign)),
            )

        def ring_arrival(h, t, way, step):
            sign = 1 if way == 0 else -1
            piece = kv[h].at[t, shard(at_z(-sign * step))]
            remote(
                piece, piece, v.ring_send.at[h, t], v.ring_recv.at[h, t, way, step - 1],
                dev(at_z(sign)),
            ).wait_recv()

        def to_sib(h, m):
            piece = kv[h].at[:, shard(m)]
            remote(piece, piece, v.sib_send.at[h], v.sib_recv.at[h], sib).start()

        def sib_all(h):
            return whole(kv[h].at[:, pl.ds(0, NZ * BLK)], v.sib_send.at[h], v.sib_recv.at[h])

        def send_own(h):
            for t in range(2):
                own[h][t].wait()
                for way in range(2):
                    ring(h, t, way, 1).start()
            to_sib(h, mem)

        def ring_step(h, step):
            for t in range(2):
                for way in range(2):
                    if step < 4 or t == way:
                        ring_arrival(h, t, way, step)
                        if step < 3 or (step == 3 and t == way):
                            ring(h, t, way, step + 1).start()
            to_sib(h, at_z(-step))
            if step < 4:
                to_sib(h, at_z(step))

        def prepare(h):
            sib_all(h).wait_recv()
            for j in range(TOPB):
                b = idx[0, 0, j]
                place(j, kv[h][0, b], kv[h][1, b])

        send_own(0)
        send_own(1)
        ring_step(0, 1)
        project(0)
        project(1)
        ring_step(0, 2)
        project(2)
        ring_step(1, 1)
        project(3)
        transposes(0)
        ring_step(0, 3)
        transposes(1)
        send_own(2)
        ring_step(0, 4)
        transposes(2)
        ring_step(1, 2)
        transposes(3)
        ready()
        prepare(0)
        part(0, 0)
        ring_step(2, 1)
        part(0, 1)
        ring_step(1, 3)
        part(0, 2)
        send_own(3)
        ring_step(1, 4)
        part(0, 3)
        ring_step(2, 2)
        prepare(1)
        part(1, 0)
        dp_start(0)
        ring_step(3, 1)
        part(1, 1)
        ring_step(2, 3)
        part(1, 2)
        ring_step(2, 4)
        part(1, 3)
        ring_step(3, 2)
        prepare(2)
        part(2, 0)
        dp_start(1)
        ring_step(3, 3)
        part(2, 1)
        part(2, 2)
        part(2, 3)
        dp_finish(0)
        ring_step(3, 4)
        tail()
        for h in range(KVH):
            for t in range(2):
                sent = kv[h].at[t, pl.ds(0, 7 * BLK)]
                whole(sent, v.ring_send.at[h, t], v.ring_recv.at[h, t, 0, 0]).wait_send()
        return

    flag = refs[9]

    def send_idx(j, m):
        remote(v.idx_own, v.idx_all.at[mem], v.misc.at[0], v.misc.at[1], dev(m)).start()

    mem_peers(send_idx)
    v.idx_all[mem] = v.idx_own[...]
    idx_seen = whole(v.idx_all.at[pl.ds(0, NMEM - 1)], v.misc.at[0], v.misc.at[1])

    def chip_copy(h):
        return remote(pool[h].at[mine], pool[h].at[mine], v.chip_send.at[h], v.chip_recv.at[h], sib)

    for h in range(KVH):
        for c in own[h]:
            c.wait()
        chip_copy(h).start()
    project(0)
    project(1)
    idx_seen.wait_recv()

    lane1 = lax.broadcasted_iota(I32, (1, 128), 1)
    home1 = lax.shift_right_logical(lane1, 3)
    lane = lax.broadcasted_iota(I32, (8, 128), 1)
    row = lax.broadcasted_iota(I32, (8, 128), 0)
    home = lax.shift_right_logical(lane, 3)
    up = jnp.zeros((1, 128), I32)
    down = jnp.zeros((1, 128), I32)
    far = jnp.zeros((1, 128), I32)
    for c in range(NZ):
        hit = jnp.maximum(
            jnp.where(v.idx_all[2 * c] == lane, 1, 0), jnp.where(v.idx_all[2 * c + 1] == lane, 1, 0)
        )
        hit = jnp.max(hit, axis=0, keepdims=True)
        d = (c - home1 + 16) & 7
        up = jnp.maximum(up, jnp.where((d >= 1) & (d <= 3), d * hit, 0))
        down = jnp.maximum(down, jnp.where(d >= 5, (8 - d) * hit, 0))
        far = jnp.maximum(far, jnp.where(d == 4, hit, 0))
    far_up = (far > 0) & ((up > down) | ((up == down) & ((lane1 & 1) == 0)))
    far_down = (far > 0) & jnp.logical_not(far_up)
    up = jnp.where(far_up, 4, up)
    down = jnp.where(far_down, 4, down)

    def follow(reach, d):
        rem = reach - d
        key = jnp.where(rem > 0, rem * 128 + 127 - lane, 0)
        since = jnp.where(d == 0, 0, 99)
        loc = jnp.where(d == 0, lane & (CHIP - 1), 0)
        sel = jnp.zeros((8, 128), I32)
        return [key, since, loc, sel]

    def step(state, t, n):
        key, since, loc, sel = state
        k = jnp.where(since <= t, key, 0)
        best = jnp.max(k, axis=1, keepdims=True)
        pick = (k == best) & (k > 0)
        key = jnp.where(pick, 0, key)
        sel = jnp.where(lane == n, jnp.max(jnp.where(pick, loc, 0), axis=1, keepdims=True), sel)
        come = pltpu.roll(jnp.where(pick, 1, 0), 1, 0) > 0
        since = jnp.where(come, t + LAG, since)
        loc = jnp.where(come, CHIP + n, loc)
        return [key, since, loc, sel]

    rings = [follow(up, (row - home + 16) & 7), follow(down, (row + home) & 7)]
    for t in range(ROUNDS):
        for w in range(WIDE):
            rings = [step(s, t, t * WIDE + w) for s in rings]
    over = jnp.maximum(rings[0][0], rings[1][0])
    over = jnp.max(jnp.max(over, axis=1, keepdims=True), axis=0, keepdims=True)
    v.flag_own[...] = jnp.broadcast_to(over, (8, 128))

    rev = lax.rem(NZ - z, NZ)

    def pick_row(x, r):
        return jnp.sum(jnp.where(row == r, x, 0), axis=0, keepdims=True)

    here = (z - home1 + 16) & 7
    loc_up = pick_row(rings[0][2], z)
    loc_down = pick_row(rings[1][2], rev)
    code = jnp.where(
        here == 0,
        lane1 & (CHIP - 1),
        jnp.where(here <= up, loc_up + SLOTS * core, loc_down + SLOTS * (1 - core)),
    )
    sel_up = pick_row(rings[0][3], z)
    sel_down = pick_row(rings[1][3], rev)
    v.work[pl.ds(0, 1), :] = code
    v.work[pl.ds(1, 1), :] = jnp.where(core == 0, sel_up, sel_down)
    v.work[pl.ds(2, 6), :] = jnp.zeros((6, 128), I32)
    to_scalars = pltpu.make_async_copy(v.work, v.tab, v.misc.at[2])
    to_scalars.start()

    def send_flag(j, d):
        remote(v.flag_own, v.flag_all.at[j - 1], v.misc.at[3], v.misc.at[4], (d, mem)).start()

    dp_peers(send_flag)
    to_scalars.wait()

    onward = dev(lax.rem(z + 1 - 2 * core + NZ, NZ) * 2 + core)

    def hop(h, t):
        return remote(
            stg[h].at[t], rcv[h].at[t], v.hop_send.at[h], v.hop_recv.at[h, t], onward
        )

    def sib_all(h):
        return whole(oth[h], v.sib_send.at[h], v.sib_recv.at[h])

    def take(h, t):
        hop(h, t).wait_recv()
        remote(
            rcv[h].at[t], oth[h].at[pl.ds(t * WIDE, WIDE)], v.sib_send.at[h], v.sib_recv.at[h], sib
        ).start()
        pool[h][pl.ds(CHIP + t * WIDE, WIDE)] = rcv[h][t]

    def round_of(h, t):
        if t == 0:
            chip_copy(h).wait_recv()
        if t >= LAG:
            take(h, t - LAG)
        for w in range(WIDE):
            stg[h][t, w] = pool[h][v.tab[1, t * WIDE + w]]
        hop(h, t).start()

    def prepare(h):
        sib_all(h).wait_recv()
        for j in range(TOPB):
            at = v.tab[0, idx[0, 0, j]]
            here_kv = pool[h][jnp.minimum(at, CHIP + SLOTS - 1)]
            there_kv = oth[h][jnp.clip(at - CHIP - SLOTS, 0, SLOTS - 1)]
            both = jnp.where(at < CHIP + SLOTS, here_kv, there_kv)
            place(j, both[0], both[1])

    half = ROUNDS // 2
    order = [(0, t) for t in range(half)]
    for h in range(KVH):
        for i in range(ROUNDS - half):
            order.append((h, half + i))
            if h + 1 < KVH and i < half:
                order.append((h + 1, i))
    work = [functools.partial(project, 2), functools.partial(project, 3)]
    work += [functools.partial(transposes, n) for n in range(4)] + [ready]
    due = {}
    for n, (h, t) in enumerate(order):
        if t == ROUNDS - 1 and h < KVH - 1:
            due.setdefault(n + 1, []).append(functools.partial(take, h, ROUNDS - 2))
            due.setdefault(n + 2, []).append(functools.partial(take, h, ROUNDS - 1))
            chunks = [functools.partial(prepare, h)]
            chunks += [functools.partial(part, h, i) for i in range(4)]
            chunks += [functools.partial(dp_start, h)] if h < 2 else []
            chunks += [functools.partial(dp_finish, 0)] if h == 2 else []
            due.setdefault(n + 4, []).append(functools.partial(work.extend, chunks))
    for n, (h, t) in enumerate(order):
        round_of(h, t)
        for action in due.pop(n, []):
            action()
        if work:
            work.pop(0)()
    take(3, ROUNDS - 2)
    take(3, ROUNDS - 1)
    for n in sorted(due):
        for action in due[n]:
            action()
    while work:
        work.pop(0)()
    tail()
    dp_seen = whole(v.flag_all, v.misc.at[3], v.misc.at[4])
    dp_seen.wait_recv()
    flag[...] = jnp.maximum(v.flag_own[...], jnp.max(v.flag_all[...], axis=0))
    for h in range(KVH):
        chip_copy(h).wait_send()
        whole(rcv[h], v.hop_send.at[h], v.hop_recv.at[h, 0]).wait_send()
    idx_seen.wait_send()
    dp_seen.wait_send()


def call(fast, args):
    hbm = pl.BlockSpec(memory_space=pl.ANY)
    vmem = pltpu.VMEM
    outs = [
        vmem((SEG, QW), BF16),
        vmem((SEG, D), BF16),
        vmem((D // (NDP * NMEM), QW), F32),
    ]
    if fast:
        outs.append(vmem((8, 128), I32))
    return pl.pallas_call(
        functools.partial(kernel, fast),
        out_shape=outs,
        in_specs=[hbm, hbm, hbm, hbm, pl.BlockSpec(memory_space=pltpu.SMEM), hbm],
        out_specs=[pl.BlockSpec(memory_space=vmem)] * len(outs),
        scratch_shapes=list((fast_scratch() if fast else slow_scratch()).values()),
        compiler_params=pltpu.CompilerParams(
            collective_id=0 if fast else 1,
            has_side_effects=True,
            vmem_limit_bytes=(58 if fast else 52) * 1024 * 1024,
        ),
    )(*args)


def on_device(*args):
    ctx, gt, gw, flag = call(True, args)
    return lax.cond(flag[0, 0] > 0, lambda: tuple(call(False, args)), lambda: (ctx, gt, gw))


def solution(mesh):
    return jax.shard_map(
        on_device,
        mesh=mesh,
        in_specs=(
            P(("dp", "mem"), None),
            P(),
            P("dp", "mem", None, None),
            P("dp", "mem", None, None),
            P("dp", "mem", None),
            P(("dp", "mem"), None),
        ),
        out_specs=(P(("dp", "mem"), None), P(("dp", "mem"), None), P(("dp", "mem"), None)),
        check_vma=False,
    )
```

```python
import functools
import math
import types

import jax
import jax.numpy as jnp
from jax import lax
from jax.experimental import pallas as pl
from jax.experimental.pallas import tpu as pltpu
from jax.sharding import PartitionSpec as P

KVH = 4
HD = 128
TOPB = 8
SEG = 512
D = 2048
QW = 1024
NZ = 8
NMEM = 16
NDP = 16
BLK = 4
CHIP = 2 * BLK
ROWS = 256
SLOTS = 17
LAG = 3
SCALE = 1.0 / HD**0.5
EXP2_SCALE = SCALE * math.log2(math.e)
MESH = pl.DeviceIdType.MESH
F32 = jnp.float32
BF16 = jnp.bfloat16
I32 = jnp.int32


def dot(a, b):
    return jnp.dot(a, b, preferred_element_type=F32)


def scratch(wanted):
    vmem, dma = pltpu.VMEM, pltpu.SemaphoreType.DMA
    table = dict(
        tok=vmem((SEG, D), BF16),
        qw=vmem((D, QW), BF16),
        dctx=vmem((SEG, QW), BF16),
        tok_t=vmem((D, SEG), BF16),
        qw_t=vmem((QW, D), BF16),
        q=vmem((KVH, SEG, 256), BF16),
        dq=vmem((KVH, SEG, 256), BF16),
        k_sel=vmem((TOPB * 128, HD), BF16),
        k_t=vmem((HD, TOPB * 128), BF16),
        v_one=vmem((TOPB * 128, 2 * HD), BF16),
        v_t=vmem((HD, TOPB * 128), BF16),
        g_keep=vmem((D, HD), F32),
        g_send=vmem((KVH, D, HD), BF16),
        g_recv=vmem((KVH, D, HD), BF16),
        g_sum=vmem((KVH, D, HD), BF16),
        dp_recv=vmem((KVH, NDP - 1, 128, HD), BF16),
        in_sem=dma((3,)),
        own_sem=dma((KVH, 2)),
        sib_send=dma((KVH,)),
        sib_recv=dma((KVH,)),
        pair_send=dma((KVH,)),
        pair_recv=dma((KVH,)),
        dp_send=dma((KVH,)),
        dp_rsem=dma((KVH,)),
        z_send=dma((2,)),
        z_rsem=dma((2,)),
    )
    table.update(wanted)
    return table


def slow_scratch():
    vmem, dma = pltpu.VMEM, pltpu.SemaphoreType.DMA
    wanted = dict(
        kv=vmem((KVH, 2, NMEM * BLK, 128, HD), BF16),
        za_send=vmem((NMEM, 8, 4 * HD), F32),
        za_recv=vmem((NMEM - 1, 8, 4 * HD), F32),
        ring_send=dma((KVH, 2)),
        ring_recv=dma((KVH, 2, 2, 4)),
    )
    return scratch(wanted)


def fast_scratch():
    vmem, dma = pltpu.VMEM, pltpu.SemaphoreType.DMA
    wanted = {}
    for h in range(KVH):
        wanted["pool%d" % h] = vmem((CHIP + SLOTS, 2, 128, HD), BF16)
        wanted["oth%d" % h] = vmem((SLOTS, 2, 128, HD), BF16)
        wanted["rcv%d" % h] = vmem((SLOTS, 2, 128, HD), BF16)
        wanted["stg%d" % h] = vmem((SLOTS, 2, 128, HD), BF16)
    wanted.update(
        za_send=vmem((NMEM, 8, 3 * HD), F32),
        za_recv=vmem((NMEM - 1, 8, 3 * HD), F32),
        zb_send=vmem((NMEM, 8, HD), F32),
        zb_recv=vmem((NMEM - 1, 8, HD), F32),
        idx_own=vmem((8, 128), I32),
        idx_all=vmem((NMEM, 8, 128), I32),
        work=vmem((8, 128), I32),
        tab=pltpu.SMEM((8, 128), I32),
        first_work=vmem((8, 128), I32),
        first_tab=pltpu.SMEM((8, 128), I32),
        flag_own=vmem((8, 128), I32),
        flag_all=vmem((NDP - 1, 8, 128), I32),
        chip_send=dma((KVH,)),
        chip_recv=dma((KVH,)),
        hop_send=dma((KVH,)),
        hop_recv=dma((KVH, SLOTS)),
        misc=dma((6,)),
    )
    return scratch(wanted)


def kernel(fast, *refs):
    tok_hbm, qw_hbm, mk_hbm, mv_hbm, idx, dctx_hbm = refs[:6]
    n_out = 4 if fast else 3
    ctx, gt, gw = refs[6:9]
    names = fast_scratch() if fast else slow_scratch()
    v = types.SimpleNamespace(**dict(zip(names, refs[6 + n_out:])))
    dp = lax.axis_index("dp")
    mem = lax.axis_index("mem")
    z = lax.div(mem, 2)
    core = lax.rem(mem, 2)

    def at_z(step):
        return lax.rem(z + step + NZ, NZ) * 2 + core

    def dev(m):
        return (dp, m)

    sib = dev(z * 2 + 1 - core)

    def shard(m):
        return pl.ds(pl.multiple_of(m * BLK, BLK), BLK)

    def remote(src, dst, send_sem, recv_sem, device):
        return pltpu.make_async_remote_copy(
            src_ref=src, dst_ref=dst, send_sem=send_sem, recv_sem=recv_sem,
            device_id=device, device_id_type=MESH,
        )

    def whole(ref, send_sem, recv_sem):
        return remote(ref, ref, send_sem, recv_sem, sib)

    def mem_peers(send):
        def body(j, carry):
            send(j, lax.rem(mem + j, NMEM))
            return carry

        lax.fori_loop(1, NMEM, body, 0)

    def dp_peers(send):
        def body(j, carry):
            send(j, lax.rem(dp + j, NDP))
            return carry

        lax.fori_loop(1, NDP, body, 0)

    if fast:
        pool = (v.pool0, v.pool1, v.pool2, v.pool3)
        oth = (v.oth0, v.oth1, v.oth2, v.oth3)
        rcv = (v.rcv0, v.rcv1, v.rcv2, v.rcv3)
        stg = (v.stg0, v.stg1, v.stg2, v.stg3)
        mine = pl.ds(pl.multiple_of(core * BLK, BLK), BLK)
        own_place = [[pool[h].at[mine, t] for t in range(2)] for h in range(KVH)]
    else:
        kv = v.kv
        own_place = [[kv.at[h, t, shard(mem)] for t in range(2)] for h in range(KVH)]

    loads = [
        pltpu.make_async_copy(tok_hbm, v.tok, v.in_sem.at[0]),
        pltpu.make_async_copy(qw_hbm, v.qw, v.in_sem.at[1]),
        pltpu.make_async_copy(dctx_hbm, v.dctx, v.in_sem.at[2]),
    ]
    own = [
        [
            pltpu.make_async_copy(
                src.at[0, :, :, pl.ds(h * HD, HD)], own_place[h][t], v.own_sem.at[h, t]
            )
            for t, src in enumerate((mk_hbm, mv_hbm))
        ]
        for h in range(KVH)
    ]
    for h in range(KVH):
        for c in own[h]:
            c.start()
    for c in loads:
        c.start()

    barrier = pltpu.get_barrier_semaphore()

    def greet(j, carry):
        pl.semaphore_signal(
            barrier, inc=1, device_id=dev(lax.rem(mem + j, NMEM)), device_id_type=MESH
        )
        pl.semaphore_signal(
            barrier, inc=1, device_id=(lax.rem(dp + j, NDP), mem), device_id_type=MESH
        )
        return carry

    lax.fori_loop(1, NMEM, greet, 0)
    if fast:
        for j in range(TOPB):
            v.idx_own[pl.ds(j, 1), :] = jnp.full((1, 128), idx[0, 0, j], I32)
    pl.semaphore_wait(barrier, 2 * (NMEM - 1))

    def at(n, size):
        return pl.ds(pl.multiple_of(n * size, size), size)

    def project(n):
        v.q[n] = dot(v.tok[...], v.qw[:, at(n, 256)]).astype(BF16)

    def transposes(n):
        v.tok_t[at(n, 512), :] = v.tok[:, at(n, 512)].T
        v.qw_t[:, at(n, 512)] = v.qw[at(n, 512), :].T

    def ready():
        loads[2].wait()
        v.v_one[:, pl.ds(HD, HD)] = jnp.ones((TOPB * 128, HD), BF16)

    def place(j, kb, vb):
        rows = pl.ds(j * 128, 128)
        v.k_sel[rows, :] = kb
        v.k_t[:, rows] = kb.T
        v.v_one[rows, pl.ds(0, HD)] = vb
        v.v_t[:, rows] = vb.T

    def attend(h, j, r):
        rows = at(r, ROWS)
        sub = at(j, HD)
        full = at(2 * h + j, HD)
        do = v.dctx[rows, full]
        s = dot(v.q[h, rows, sub], v.k_t[...])
        top = jnp.max(s, axis=-1, keepdims=True)
        e = jnp.exp2((s - top) * EXP2_SCALE)
        pv = dot(e.astype(BF16), v.v_one[...])
        inv = 1.0 / pv[:, HD:]
        c = pv[:, :HD] * inv
        ctx[rows, full] = c.astype(BF16)
        d_p = dot(do, v.v_t[...])
        delta = jnp.sum(do.astype(F32) * c, axis=-1, keepdims=True)
        ds = (e * (d_p - delta)).astype(BF16)
        v.dq[h, rows, sub] = (dot(ds, v.k_sel[...]) * (inv * SCALE)).astype(BF16)

    def weight_grad(h, first):
        j = 1 - core if first else core
        sub = pl.ds(pl.multiple_of(j * HD, HD), HD)

        def tile(i, carry):
            rows = pl.ds(pl.multiple_of(i * 1024, 1024), 1024)
            g = dot(v.tok_t[rows, :], v.dq[h, :, sub])
            if first:
                v.g_send[h, rows, :] = g.astype(BF16)
            else:
                v.g_keep[rows, :] = g
            return carry

        lax.fori_loop(0, D // 1024, tile, 0)
        if first:
            pair(h).start()

    def part(h, n):
        attend(h, 1 - core if n < 2 else core, n % 2)
        if n % 2 == 1:
            weight_grad(h, n < 2)

    def pair(h):
        return remote(v.g_send.at[h], v.g_recv.at[h], v.pair_send.at[h], v.pair_recv.at[h], sib)

    def dp_start(h):
        pair(h).wait_recv()

        def tile(i, carry):
            rows = pl.ds(pl.multiple_of(i * 256, 256), 256)
            total = v.g_keep[rows, :] + v.g_recv[h, rows, :].astype(F32)
            v.g_sum[h, rows, :] = total.astype(BF16)
            return carry

        lax.fori_loop(0, D // 256, tile, 0)

        def send(j, d):
            rows = pl.ds(pl.multiple_of(d * 128, 128), 128)
            remote(
                v.g_sum.at[h, rows], v.dp_recv.at[h, j - 1], v.dp_send.at[h], v.dp_rsem.at[h],
                (d, mem),
            ).start()

        dp_peers(send)

    def dp_all(h):
        return whole(v.dp_recv.at[h], v.dp_send.at[h], v.dp_rsem.at[h])

    def dp_finish(h, dst, n):
        dp_all(h).wait_recv()
        acc = v.g_sum[h, at(dp, 128), :].astype(F32)
        for j in range(NDP - 1):
            acc = acc + v.dp_recv[h, j].astype(F32)
        dst[:, :, at(n, HD)] = acc.reshape(NMEM, 8, HD)

    def z_start(n, src, dst):
        def send(j, m):
            remote(src.at[m], dst.at[j - 1], v.z_send.at[n], v.z_rsem.at[n], dev(m)).start()

        mem_peers(send)

    def z_all(n, dst):
        return whole(dst, v.z_send.at[n], v.z_rsem.at[n])

    def z_finish(n, src, dst, heads):
        z_all(n, dst).wait_recv()
        same = src[mem]
        other = dst[0]
        for j in range(2, NMEM):
            if j % 2 == 0:
                same = same + dst[j - 1]
            else:
                other = other + dst[j - 1]
        for i, h in enumerate(heads):
            cut = slice(i * HD, (i + 1) * HD)
            gw[:, pl.ds(pl.multiple_of(h * 256 + core * HD, HD), HD)] = same[:, cut]
            gw[:, pl.ds(pl.multiple_of(h * 256 + (1 - core) * HD, HD), HD)] = other[:, cut]

    def grad_tokens():
        def tile(n, carry):
            cols = at(n, 512)
            acc = dot(v.dq[0], v.qw_t[pl.ds(0, 256), cols])
            for h in range(1, KVH):
                acc = acc + dot(v.dq[h], v.qw_t[pl.ds(h * 256, 256), cols])
            gt[:, cols] = acc.astype(BF16)
            return carry

        lax.fori_loop(0, D // 512, tile, 0)

    def each(n, body):
        def run(i, carry):
            body(i)
            return carry

        lax.fori_loop(0, n, run, 0)

    def sent_all():
        for h in range(KVH):
            sib_all(h).wait_send()
            pair(h).wait_send()
            dp_all(h).wait_send()
        z_all(0, v.za_recv).wait_send()

    if not fast:
        def ring(h, t, way, step, back):
            sign = 1 if way == 0 else -1
            piece = kv.at[h, t, shard(at_z(-sign * back))]
            return remote(
                piece, piece, v.ring_send.at[h, t], v.ring_recv.at[h, t, way, step - 1],
                dev(at_z(sign)),
            )

        def to_sib(h, m):
            piece = kv.at[h, :, shard(m)]
            remote(piece, piece, v.sib_send.at[h], v.sib_recv.at[h], sib).start()

        def sib_all(h):
            return whole(kv.at[h, :, pl.ds(0, NZ * BLK)], v.sib_send.at[h], v.sib_recv.at[h])

        def send_own(h):
            for t in range(2):
                for way in range(2):
                    ring(h, t, way, 1, 0).start()
            to_sib(h, mem)

        def ring_step(h, step):
            for t in range(2):
                for way in range(2):
                    if step < 4 or t == way:
                        ring(h, t, way, step, step).wait_recv()
                        if step < 3 or (step == 3 and t == way):
                            ring(h, t, way, step + 1, step).start()
            to_sib(h, at_z(-step))
            if step < 4:
                to_sib(h, at_z(step))

        def head(h):
            for j in range(TOPB):
                b = idx[0, 0, j]
                place(j, kv[h, 0, b], kv[h, 1, b])

            def quarter(n):
                attend(h, lax.rem(1 - core + lax.div(n, 2), 2), lax.rem(n, 2))

            each(4, quarter)
            weight_grad(h, True)
            weight_grad(h, False)
            dp_start(h)
            dp_finish(h, v.za_send, h)

        for h in range(KVH):
            for c in own[h]:
                c.wait()
        each(KVH, send_own)
        for step in range(1, 5):
            each(KVH, functools.partial(ring_step, step=step))
        loads[0].wait()
        loads[1].wait()
        each(KVH, project)
        each(KVH, transposes)
        ready()
        for h in range(KVH):
            sib_all(h).wait_recv()
        each(KVH, head)
        z_start(0, v.za_send, v.za_recv)
        grad_tokens()
        z_finish(0, v.za_send, v.za_recv, (0, 1, 2, 3))
        sent_all()
        for h in range(KVH):
            for t in range(2):
                sent = kv.at[h, t, pl.ds(0, 7 * BLK)]
                whole(sent, v.ring_send.at[h, t], v.ring_recv.at[h, t, 0, 0]).wait_send()
        return

    flag = refs[9]

    def send_idx(j, m):
        remote(v.idx_own, v.idx_all.at[mem], v.misc.at[0], v.misc.at[1], dev(m)).start()

    mem_peers(send_idx)
    v.idx_all[mem] = v.idx_own[...]
    idx_seen = whole(v.idx_all.at[pl.ds(0, NMEM - 1)], v.misc.at[0], v.misc.at[1])

    def chip_copy(h):
        return remote(pool[h].at[mine], pool[h].at[mine], v.chip_send.at[h], v.chip_recv.at[h], sib)

    for h in range(KVH):
        for c in own[h]:
            c.wait()
        chip_copy(h).start()
    loads[0].wait()
    loads[1].wait()
    project(0)
    project(1)
    idx_seen.wait_recv()

    lane1 = lax.broadcasted_iota(I32, (1, 128), 1)
    home1 = lax.shift_right_logical(lane1, 3)
    lane = lax.broadcasted_iota(I32, (8, 128), 1)
    row = lax.broadcasted_iota(I32, (8, 128), 0)
    home = lax.shift_right_logical(lane, 3)
    up = jnp.zeros((1, 128), I32)
    down = jnp.zeros((1, 128), I32)
    far = jnp.zeros((1, 128), I32)
    for c in range(NZ):
        hit = jnp.maximum(
            jnp.where(v.idx_all[2 * c] == lane, 1, 0), jnp.where(v.idx_all[2 * c + 1] == lane, 1, 0)
        )
        hit = jnp.max(hit, axis=0, keepdims=True)
        d = (c - home1 + 16) & 7
        up = jnp.maximum(up, jnp.where((d >= 1) & (d <= 3), d * hit, 0))
        down = jnp.maximum(down, jnp.where(d >= 5, (8 - d) * hit, 0))
        far = jnp.maximum(far, jnp.where(d == 4, hit, 0))

    def load(reach, d):
        return jnp.sum(jnp.where(d < reach, 1, 0), axis=1, keepdims=True)

    def worst(load_of, reach, d):
        return jnp.max(jnp.where((d >= reach) & (d < 4), load_of, 0), axis=0, keepdims=True)

    d_up = (row - home + 16) & 7
    d_down = (home - row + 16) & 7
    up3, down3 = up, down
    for k in range(4):
        cost_up = 4 * worst(load(up, d_up), up3, d_up) + 3 - up3
        cost_down = 4 * worst(load(down, d_down), down3, d_down) + 3 - down3
        upward = (cost_up < cost_down) | ((cost_up == cost_down) & ((lane1 & 4) == 0))
        lot = (far > 0) & ((lane1 & 3) == k)
        up = jnp.where(lot & upward, 4, up)
        down = jnp.where(lot & jnp.logical_not(upward), 4, down)

    def follow(reach, d):
        rem = reach - d
        key = jnp.where(rem > 0, rem * 128 + 127 - lane, 0)
        since = jnp.where(d == 0, 0, 99)
        loc = jnp.where(d == 0, lane & (CHIP - 1), 0)
        sel = jnp.zeros((8, 128), I32)
        return [key, since, loc, sel]

    def step(state, t):
        key, since, loc, sel = state
        k = jnp.where(since <= t, key, 0)
        best = jnp.max(k, axis=1, keepdims=True)
        pick = (k == best) & (k > 0)
        key = jnp.where(pick, 0, key)
        sel = jnp.where(lane == t, jnp.max(jnp.where(pick, loc, 0), axis=1, keepdims=True), sel)
        come = pltpu.roll(jnp.where(pick, 1, 0), 1, 0) > 0
        since = jnp.where(come, t + LAG, since)
        loc = jnp.where(come, CHIP + t, loc)
        return [key, since, loc, sel]

    rings = [follow(up, d_up), follow(down, (row + home) & 7)]
    rev = lax.rem(NZ - z, NZ)

    def pick_row(x, r):
        return jnp.sum(jnp.where(row == r, x, 0), axis=0, keepdims=True)

    onward = dev(lax.rem(z + 1 - 2 * core + NZ, NZ) * 2 + core)

    def hop(h, t):
        return remote(
            stg[h].at[t], rcv[h].at[t], v.hop_send.at[h], v.hop_recv.at[h, t], onward
        )

    def sib_all(h):
        return whole(oth[h], v.sib_send.at[h], v.sib_recv.at[h])

    def take(h, t):
        hop(h, t).wait_recv()
        remote(rcv[h].at[t], oth[h].at[t], v.sib_send.at[h], v.sib_recv.at[h], sib).start()
        pool[h][CHIP + t] = rcv[h][t]

    def round_of(h, t):
        if t == 0:
            chip_copy(h).wait_recv()
        if t >= LAG:
            take(h, t - LAG)
        chosen = v.first_tab[0, t] if h == 0 and t < LAG else v.tab[1, t]
        stg[h][t] = pool[h][chosen]
        hop(h, t).start()

    for t in range(LAG):
        rings = [step(s, t) for s in rings]

    def my_picks():
        picks = jnp.where(core == 0, pick_row(rings[0][3], z), pick_row(rings[1][3], rev))
        return jnp.broadcast_to(picks, (8, 128))

    v.first_work[...] = my_picks()
    to_first = pltpu.make_async_copy(v.first_work, v.first_tab, v.misc.at[5])
    to_first.start()
    to_first.wait()
    for t in range(LAG):
        round_of(0, t)
    for t in range(LAG, SLOTS):
        rings = [step(s, t) for s in rings]
    over = jnp.maximum(rings[0][0], rings[1][0])
    over = jnp.max(jnp.max(over, axis=1, keepdims=True), axis=0, keepdims=True)
    v.flag_own[...] = jnp.broadcast_to(over, (8, 128))

    here = (z - home1 + 16) & 7
    loc_up = pick_row(rings[0][2], z)
    loc_down = pick_row(rings[1][2], rev)
    code = jnp.where(
        here == 0,
        lane1 & (CHIP - 1),
        jnp.where(here <= up, loc_up + SLOTS * core, loc_down + SLOTS * (1 - core)),
    )
    v.work[...] = my_picks()
    v.work[pl.ds(0, 1), :] = code
    to_scalars = pltpu.make_async_copy(v.work, v.tab, v.misc.at[2])
    to_scalars.start()

    def send_flag(j, d):
        remote(v.flag_own, v.flag_all.at[j - 1], v.misc.at[3], v.misc.at[4], (d, mem)).start()

    dp_peers(send_flag)
    to_scalars.wait()

    def prepare(h):
        sib_all(h).wait_recv()
        for j in range(TOPB):
            spot = v.tab[0, idx[0, 0, j]]
            here_kv = pool[h][jnp.minimum(spot, CHIP + SLOTS - 1)]
            there_kv = oth[h][jnp.clip(spot - CHIP - SLOTS, 0, SLOTS - 1)]
            both = jnp.where(spot < CHIP + SLOTS, here_kv, there_kv)
            place(j, both[0], both[1])

    half = SLOTS // 2
    order = [(0, t) for t in range(LAG, half)]
    for h in range(KVH):
        for i in range(SLOTS - half):
            order.append((h, half + i))
            if h + 1 < KVH and i < half:
                order.append((h + 1, i))
    work = [functools.partial(project, 2), functools.partial(project, 3)]
    work += [functools.partial(transposes, n) for n in range(4)] + [ready]
    due = {}
    for n, (h, t) in enumerate(order):
        if t == SLOTS - 1 and h < KVH - 1:
            for i in range(LAG):
                due.setdefault(n + 1 + i, []).append(functools.partial(take, h, SLOTS - LAG + i))
            chunks = [functools.partial(prepare, h)]
            chunks += [functools.partial(part, h, i) for i in range(4)]
            chunks += [functools.partial(dp_start, h)]
            if h == 2:
                chunks += [functools.partial(dp_finish, 0, v.za_send, 0)]
            due.setdefault(n + (5 if h == 2 else 6), []).append(functools.partial(work.extend, chunks))
    for n, (h, t) in enumerate(order):
        round_of(h, t)
        for action in due.pop(n, []):
            action()
        if work and (n % 2 == 1 or n < half or h == 3 and t >= half):
            work.pop(0)()
    for t in range(SLOTS - LAG, SLOTS):
        if work:
            work.pop(0)()
        take(3, t)
    for n in sorted(due):
        for action in due[n]:
            action()
    while work:
        work.pop(0)()
    prepare(3)
    for n in range(4):
        part(3, n)
    dp_start(3)
    dp_finish(1, v.za_send, 1)
    dp_finish(2, v.za_send, 2)
    z_start(0, v.za_send, v.za_recv)
    grad_tokens()
    z_finish(0, v.za_send, v.za_recv, (0, 1, 2))
    dp_finish(3, v.zb_send, 0)
    z_start(1, v.zb_send, v.zb_recv)
    z_finish(1, v.zb_send, v.zb_recv, (3,))
    sent_all()
    z_all(1, v.zb_recv).wait_send()
    dp_seen = whole(v.flag_all, v.misc.at[3], v.misc.at[4])
    dp_seen.wait_recv()
    flag[...] = jnp.maximum(v.flag_own[...], jnp.max(v.flag_all[...], axis=0))
    for h in range(KVH):
        chip_copy(h).wait_send()
        whole(rcv[h], v.hop_send.at[h], v.hop_recv.at[h, 0]).wait_send()
    idx_seen.wait_send()
    dp_seen.wait_send()


def call(fast, args):
    hbm = pl.BlockSpec(memory_space=pl.ANY)
    vmem = pltpu.VMEM
    outs = [
        vmem((SEG, QW), BF16),
        vmem((SEG, D), BF16),
        vmem((D // (NDP * NMEM), QW), F32),
    ]
    if fast:
        outs.append(vmem((8, 128), I32))
    return pl.pallas_call(
        functools.partial(kernel, fast),
        out_shape=outs,
        in_specs=[hbm, hbm, hbm, hbm, pl.BlockSpec(memory_space=pltpu.SMEM), hbm],
        out_specs=[pl.BlockSpec(memory_space=vmem)] * len(outs),
        scratch_shapes=list((fast_scratch() if fast else slow_scratch()).values()),
        compiler_params=pltpu.CompilerParams(
            collective_id=0 if fast else 1,
            has_side_effects=True,
            vmem_limit_bytes=(58 if fast else 52) * 1024 * 1024,
        ),
    )(*args)


def store(*refs):
    copies = [
        pltpu.make_async_copy(src, dst, refs[6].at[i])
        for i, (src, dst) in enumerate(zip(refs[:3], refs[3:6]))
    ]
    for c in copies:
        c.start()
    for c in copies:
        c.wait()


def on_device(*args):
    ctx, gt, gw, flag = call(True, args)
    outs = lax.cond(flag[0, 0] > 0, lambda: tuple(call(False, args)), lambda: (ctx, gt, gw))
    hbm = pl.BlockSpec(memory_space=pl.ANY)
    return pl.pallas_call(
        store,
        out_shape=[jax.ShapeDtypeStruct(x.shape, x.dtype) for x in outs],
        in_specs=[hbm] * 3,
        out_specs=[hbm] * 3,
        scratch_shapes=[pltpu.SemaphoreType.DMA((3,))],
    )(*outs)


def solution(mesh):
    return jax.shard_map(
        on_device,
        mesh=mesh,
        in_specs=(
            P(("dp", "mem"), None),
            P(),
            P("dp", "mem", None, None),
            P("dp", "mem", None, None),
            P("dp", "mem", None),
            P(("dp", "mem"), None),
        ),
        out_specs=(P(("dp", "mem"), None), P(("dp", "mem"), None), P(("dp", "mem"), None)),
        check_vma=False,
    )
```

```python
import functools
import math
import types

import jax
import jax.numpy as jnp
from jax import lax
from jax.experimental import pallas as pl
from jax.experimental.pallas import tpu as pltpu
from jax.sharding import PartitionSpec as P

KVH = 4
HD = 128
TOPB = 8
SEG = 512
D = 2048
QW = 1024
NZ = 8
NMEM = 16
NDP = 16
BLK = 4
CHIP = 2 * BLK
ROWS = 256
SLOTS = 17
LAG = 3
SCALE = 1.0 / HD**0.5
EXP2_SCALE = SCALE * math.log2(math.e)
MESH = pl.DeviceIdType.MESH
F32 = jnp.float32
BF16 = jnp.bfloat16
I32 = jnp.int32


def dot(a, b):
    return jnp.dot(a, b, preferred_element_type=F32)


def scratch(wanted):
    vmem, dma = pltpu.VMEM, pltpu.SemaphoreType.DMA
    table = dict(
        tok=vmem((SEG, D), BF16),
        qw=vmem((D, QW), BF16),
        dctx=vmem((SEG, QW), BF16),
        tok_t=vmem((D, SEG), BF16),
        qw_t=vmem((QW, D), BF16),
        q=vmem((KVH, SEG, 256), BF16),
        dq=vmem((KVH, SEG, 256), BF16),
        k_sel=vmem((TOPB * 128, HD), BF16),
        k_t=vmem((HD, TOPB * 128), BF16),
        v_one=vmem((TOPB * 128, 2 * HD), BF16),
        v_t=vmem((HD, TOPB * 128), BF16),
        g_keep=vmem((D, HD), F32),
        g_send=vmem((KVH, D, HD), BF16),
        g_recv=vmem((KVH, D, HD), BF16),
        g_sum=vmem((KVH, D, HD), BF16),
        dp_recv=vmem((KVH, NDP - 1, 128, HD), BF16),
        in_sem=dma((3,)),
        own_sem=dma((KVH, 2)),
        sib_send=dma((KVH,)),
        sib_recv=dma((KVH,)),
        pair_send=dma((KVH,)),
        pair_recv=dma((KVH,)),
        dp_send=dma((KVH,)),
        dp_rsem=dma((KVH,)),
        z_send=dma((2,)),
        z_rsem=dma((2,)),
    )
    table.update(wanted)
    return table


def slow_scratch():
    vmem, dma = pltpu.VMEM, pltpu.SemaphoreType.DMA
    wanted = dict(
        kv=vmem((KVH, 2, NMEM * BLK, 128, HD), BF16),
        za_send=vmem((NMEM, 8, 4 * HD), F32),
        za_recv=vmem((NMEM - 1, 8, 4 * HD), F32),
        ring_send=dma((KVH, 2)),
        ring_recv=dma((KVH, 2, 2, 4)),
    )
    return scratch(wanted)


def fast_scratch():
    vmem, dma = pltpu.VMEM, pltpu.SemaphoreType.DMA
    wanted = {}
    for h in range(KVH):
        wanted["pool%d" % h] = vmem((CHIP + SLOTS, 2, 128, HD), BF16)
        wanted["oth%d" % h] = vmem((SLOTS, 2, 128, HD), BF16)
        wanted["rcv%d" % h] = vmem((SLOTS, 2, 128, HD), BF16)
        wanted["stg%d" % h] = vmem((SLOTS, 2, 128, HD), BF16)
    wanted.update(
        za_send=vmem((NMEM, 8, 3 * HD), F32),
        za_recv=vmem((NMEM - 1, 8, 3 * HD), F32),
        zb_send=vmem((NMEM, 8, HD), F32),
        zb_recv=vmem((NMEM - 1, 8, HD), F32),
        idx_own=vmem((8, 128), I32),
        idx_all=vmem((NMEM, 8, 128), I32),
        work=vmem((8, 128), I32),
        tab=pltpu.SMEM((8, 128), I32),
        first_work=vmem((8, 128), I32),
        first_tab=pltpu.SMEM((8, 128), I32),
        flag_own=vmem((8, 128), I32),
        flag_all=vmem((NDP - 1, 8, 128), I32),
        chip_send=dma((KVH,)),
        chip_recv=dma((KVH,)),
        hop_send=dma((KVH,)),
        hop_recv=dma((KVH, SLOTS)),
        misc=dma((6,)),
    )
    return scratch(wanted)


def kernel(fast, *refs):
    tok_hbm, qw_hbm, mk_hbm, mv_hbm, idx, dctx_hbm = refs[:6]
    n_out = 4 if fast else 3
    ctx, gt, gw = refs[6:9]
    names = fast_scratch() if fast else slow_scratch()
    v = types.SimpleNamespace(**dict(zip(names, refs[6 + n_out:])))
    dp = lax.axis_index("dp")
    mem = lax.axis_index("mem")
    z = lax.div(mem, 2)
    core = lax.rem(mem, 2)

    def at_z(step):
        return lax.rem(z + step + NZ, NZ) * 2 + core

    def dev(m):
        return (dp, m)

    sib = dev(z * 2 + 1 - core)

    def shard(m):
        return pl.ds(pl.multiple_of(m * BLK, BLK), BLK)

    def remote(src, dst, send_sem, recv_sem, device):
        return pltpu.make_async_remote_copy(
            src_ref=src, dst_ref=dst, send_sem=send_sem, recv_sem=recv_sem,
            device_id=device, device_id_type=MESH,
        )

    def whole(ref, send_sem, recv_sem):
        return remote(ref, ref, send_sem, recv_sem, sib)

    def mem_peers(send):
        def body(j, carry):
            send(j, lax.rem(mem + j, NMEM))
            return carry

        lax.fori_loop(1, NMEM, body, 0)

    def dp_peers(send):
        def body(j, carry):
            send(j, lax.rem(dp + j, NDP))
            return carry

        lax.fori_loop(1, NDP, body, 0)

    if fast:
        pool = (v.pool0, v.pool1, v.pool2, v.pool3)
        oth = (v.oth0, v.oth1, v.oth2, v.oth3)
        rcv = (v.rcv0, v.rcv1, v.rcv2, v.rcv3)
        stg = (v.stg0, v.stg1, v.stg2, v.stg3)
        mine = pl.ds(pl.multiple_of(core * BLK, BLK), BLK)
        own_place = [[pool[h].at[mine, t] for t in range(2)] for h in range(KVH)]
    else:
        kv = v.kv
        own_place = [[kv.at[h, t, shard(mem)] for t in range(2)] for h in range(KVH)]

    loads = [
        pltpu.make_async_copy(tok_hbm, v.tok, v.in_sem.at[0]),
        pltpu.make_async_copy(qw_hbm, v.qw, v.in_sem.at[1]),
        pltpu.make_async_copy(dctx_hbm, v.dctx, v.in_sem.at[2]),
    ]
    own = [
        [
            pltpu.make_async_copy(
                src.at[0, :, :, pl.ds(h * HD, HD)], own_place[h][t], v.own_sem.at[h, t]
            )
            for t, src in enumerate((mk_hbm, mv_hbm))
        ]
        for h in range(KVH)
    ]
    for h in range(KVH):
        for c in own[h]:
            c.start()
    for c in loads:
        c.start()

    barrier = pltpu.get_barrier_semaphore()

    def greet(j, carry):
        pl.semaphore_signal(
            barrier, inc=1, device_id=dev(lax.rem(mem + j, NMEM)), device_id_type=MESH
        )
        pl.semaphore_signal(
            barrier, inc=1, device_id=(lax.rem(dp + j, NDP), mem), device_id_type=MESH
        )
        return carry

    lax.fori_loop(1, NMEM, greet, 0)
    if fast:
        for j in range(TOPB):
            v.idx_own[pl.ds(j, 1), :] = jnp.full((1, 128), idx[0, 0, j], I32)
    pl.semaphore_wait(barrier, 2 * (NMEM - 1))

    def at(n, size):
        return pl.ds(pl.multiple_of(n * size, size), size)

    def project(n):
        v.q[n] = dot(v.tok[...], v.qw[:, at(n, 256)]).astype(BF16)

    def transposes(n):
        v.tok_t[at(n, 512), :] = v.tok[:, at(n, 512)].T
        v.qw_t[:, at(n, 512)] = v.qw[at(n, 512), :].T

    def ready():
        loads[2].wait()
        v.v_one[:, pl.ds(HD, HD)] = jnp.ones((TOPB * 128, HD), BF16)

    def place(j, kb, vb):
        rows = pl.ds(j * 128, 128)
        v.k_sel[rows, :] = kb
        v.k_t[:, rows] = kb.T
        v.v_one[rows, pl.ds(0, HD)] = vb
        v.v_t[:, rows] = vb.T

    def attend(h, j, r):
        rows = at(r, ROWS)
        sub = at(j, HD)
        full = at(2 * h + j, HD)
        do = v.dctx[rows, full]
        s = dot(v.q[h, rows, sub], v.k_t[...])
        top = jnp.max(s, axis=-1, keepdims=True)
        e = jnp.exp2((s - top) * EXP2_SCALE)
        pv = dot(e.astype(BF16), v.v_one[...])
        inv = 1.0 / pv[:, HD:]
        c = pv[:, :HD] * inv
        ctx[rows, full] = c.astype(BF16)
        d_p = dot(do, v.v_t[...])
        delta = jnp.sum(do.astype(F32) * c, axis=-1, keepdims=True)
        ds = (e * (d_p - delta)).astype(BF16)
        v.dq[h, rows, sub] = (dot(ds, v.k_sel[...]) * (inv * SCALE)).astype(BF16)

    def weight_grad(h, first):
        j = 1 - core if first else core
        sub = pl.ds(pl.multiple_of(j * HD, HD), HD)

        def tile(i, carry):
            rows = pl.ds(pl.multiple_of(i * 1024, 1024), 1024)
            g = dot(v.tok_t[rows, :], v.dq[h, :, sub])
            if first:
                v.g_send[h, rows, :] = g.astype(BF16)
            else:
                v.g_keep[rows, :] = g
            return carry

        lax.fori_loop(0, D // 1024, tile, 0)
        if first:
            pair(h).start()

    def part(h, n):
        attend(h, 1 - core if n < 2 else core, n % 2)
        if n % 2 == 1:
            weight_grad(h, n < 2)

    def pair(h):
        return remote(v.g_send.at[h], v.g_recv.at[h], v.pair_send.at[h], v.pair_recv.at[h], sib)

    def dp_start(h):
        pair(h).wait_recv()

        def add_up(d):
            rows = at(d, 128)
            total = v.g_keep[rows, :] + v.g_recv[h, rows, :].astype(F32)
            v.g_sum[h, rows, :] = total.astype(BF16)

        def send(j, d):
            add_up(d)
            remote(
                v.g_sum.at[h, at(d, 128)], v.dp_recv.at[h, j - 1], v.dp_send.at[h], v.dp_rsem.at[h],
                (d, mem),
            ).start()

        dp_peers(send)
        add_up(dp)

    def dp_all(h):
        return whole(v.dp_recv.at[h], v.dp_send.at[h], v.dp_rsem.at[h])

    def dp_finish(h, dst, n):
        dp_all(h).wait_recv()
        acc = v.g_sum[h, at(dp, 128), :].astype(F32)
        for j in range(NDP - 1):
            acc = acc + v.dp_recv[h, j].astype(F32)
        dst[:, :, at(n, HD)] = acc.reshape(NMEM, 8, HD)

    def z_start(n, src, dst):
        def send(j, m):
            remote(src.at[m], dst.at[j - 1], v.z_send.at[n], v.z_rsem.at[n], dev(m)).start()

        mem_peers(send)

    def z_all(n, dst):
        return whole(dst, v.z_send.at[n], v.z_rsem.at[n])

    def z_finish(n, src, dst, heads):
        z_all(n, dst).wait_recv()
        same = src[mem]
        other = dst[0]
        for j in range(2, NMEM):
            if j % 2 == 0:
                same = same + dst[j - 1]
            else:
                other = other + dst[j - 1]
        for i, h in enumerate(heads):
            cut = slice(i * HD, (i + 1) * HD)
            gw[:, pl.ds(pl.multiple_of(h * 256 + core * HD, HD), HD)] = same[:, cut]
            gw[:, pl.ds(pl.multiple_of(h * 256 + (1 - core) * HD, HD), HD)] = other[:, cut]

    def grad_tokens():
        def tile(n, carry):
            cols = at(n, 512)
            acc = dot(v.dq[0], v.qw_t[pl.ds(0, 256), cols])
            for h in range(1, KVH):
                acc = acc + dot(v.dq[h], v.qw_t[pl.ds(h * 256, 256), cols])
            gt[:, cols] = acc.astype(BF16)
            return carry

        lax.fori_loop(0, D // 512, tile, 0)

    def each(n, body):
        def run(i, carry):
            body(i)
            return carry

        lax.fori_loop(0, n, run, 0)

    def sent_all():
        for h in range(KVH):
            sib_all(h).wait_send()
            pair(h).wait_send()
            dp_all(h).wait_send()
        z_all(0, v.za_recv).wait_send()

    if not fast:
        def ring(h, t, way, step, back):
            sign = 1 if way == 0 else -1
            piece = kv.at[h, t, shard(at_z(-sign * back))]
            return remote(
                piece, piece, v.ring_send.at[h, t], v.ring_recv.at[h, t, way, step - 1],
                dev(at_z(sign)),
            )

        def to_sib(h, m):
            piece = kv.at[h, :, shard(m)]
            remote(piece, piece, v.sib_send.at[h], v.sib_recv.at[h], sib).start()

        def sib_all(h):
            return whole(kv.at[h, :, pl.ds(0, NZ * BLK)], v.sib_send.at[h], v.sib_recv.at[h])

        def send_own(h):
            for t in range(2):
                for way in range(2):
                    ring(h, t, way, 1, 0).start()
            to_sib(h, mem)

        def ring_step(h, step):
            for t in range(2):
                for way in range(2):
                    if step < 4 or t == way:
                        ring(h, t, way, step, step).wait_recv()
                        if step < 3 or (step == 3 and t == way):
                            ring(h, t, way, step + 1, step).start()
            to_sib(h, at_z(-step))
            if step < 4:
                to_sib(h, at_z(step))

        def head(h):
            for j in range(TOPB):
                b = idx[0, 0, j]
                place(j, kv[h, 0, b], kv[h, 1, b])

            def quarter(n):
                attend(h, lax.rem(1 - core + lax.div(n, 2), 2), lax.rem(n, 2))

            each(4, quarter)
            weight_grad(h, True)
            weight_grad(h, False)
            dp_start(h)
            dp_finish(h, v.za_send, h)

        for h in range(KVH):
            for c in own[h]:
                c.wait()
        each(KVH, send_own)
        for step in range(1, 5):
            each(KVH, functools.partial(ring_step, step=step))
        loads[0].wait()
        loads[1].wait()
        each(KVH, project)
        each(KVH, transposes)
        ready()
        for h in range(KVH):
            sib_all(h).wait_recv()
        each(KVH, head)
        z_start(0, v.za_send, v.za_recv)
        grad_tokens()
        z_finish(0, v.za_send, v.za_recv, (0, 1, 2, 3))
        sent_all()
        for h in range(KVH):
            for t in range(2):
                sent = kv.at[h, t, pl.ds(0, 7 * BLK)]
                whole(sent, v.ring_send.at[h, t], v.ring_recv.at[h, t, 0, 0]).wait_send()
        return

    flag = refs[9]

    def send_idx(j, m):
        remote(v.idx_own, v.idx_all.at[mem], v.misc.at[0], v.misc.at[1], dev(m)).start()

    mem_peers(send_idx)
    v.idx_all[mem] = v.idx_own[...]
    idx_seen = whole(v.idx_all.at[pl.ds(0, NMEM - 1)], v.misc.at[0], v.misc.at[1])

    def chip_copy(h):
        return remote(pool[h].at[mine], pool[h].at[mine], v.chip_send.at[h], v.chip_recv.at[h], sib)

    for h in range(KVH):
        for c in own[h]:
            c.wait()
        chip_copy(h).start()
    loads[0].wait()
    loads[1].wait()
    project(0)
    project(1)
    idx_seen.wait_recv()

    lane1 = lax.broadcasted_iota(I32, (1, 128), 1)
    home1 = lax.shift_right_logical(lane1, 3)
    lane = lax.broadcasted_iota(I32, (8, 128), 1)
    row = lax.broadcasted_iota(I32, (8, 128), 0)
    home = lax.shift_right_logical(lane, 3)
    up = jnp.zeros((1, 128), I32)
    down = jnp.zeros((1, 128), I32)
    far = jnp.zeros((1, 128), I32)
    for c in range(NZ):
        hit = jnp.maximum(
            jnp.where(v.idx_all[2 * c] == lane, 1, 0), jnp.where(v.idx_all[2 * c + 1] == lane, 1, 0)
        )
        hit = jnp.max(hit, axis=0, keepdims=True)
        d = (c - home1 + 16) & 7
        up = jnp.maximum(up, jnp.where((d >= 1) & (d <= 3), d * hit, 0))
        down = jnp.maximum(down, jnp.where(d >= 5, (8 - d) * hit, 0))
        far = jnp.maximum(far, jnp.where(d == 4, hit, 0))

    def load(reach, d):
        return jnp.sum(jnp.where(d < reach, 1, 0), axis=1, keepdims=True)

    def worst(load_of, reach, d):
        return jnp.max(jnp.where((d >= reach) & (d < 4), load_of, 0), axis=0, keepdims=True)

    d_up = (row - home + 16) & 7
    d_down = (home - row + 16) & 7
    up3, down3 = up, down
    for k in range(4):
        cost_up = 4 * worst(load(up, d_up), up3, d_up) + 3 - up3
        cost_down = 4 * worst(load(down, d_down), down3, d_down) + 3 - down3
        upward = (cost_up < cost_down) | ((cost_up == cost_down) & ((lane1 & 4) == 0))
        lot = (far > 0) & ((lane1 & 3) == k)
        up = jnp.where(lot & upward, 4, up)
        down = jnp.where(lot & jnp.logical_not(upward), 4, down)

    def follow(reach, d):
        rem = reach - d
        key = jnp.where(rem > 0, rem * 128 + 127 - lane, 0)
        since = jnp.where(d == 0, 0, 99)
        loc = jnp.where(d == 0, lane & (CHIP - 1), 0)
        sel = jnp.zeros((8, 128), I32)
        return [key, since, loc, sel]

    def step(state, t):
        key, since, loc, sel = state
        k = jnp.where(since <= t, key, 0)
        best = jnp.max(k, axis=1, keepdims=True)
        pick = (k == best) & (k > 0)
        key = jnp.where(pick, 0, key)
        sel = jnp.where(lane == t, jnp.max(jnp.where(pick, loc, 0), axis=1, keepdims=True), sel)
        come = pltpu.roll(jnp.where(pick, 1, 0), 1, 0) > 0
        since = jnp.where(come, t + LAG, since)
        loc = jnp.where(come, CHIP + t, loc)
        return [key, since, loc, sel]

    rings = [follow(up, d_up), follow(down, (row + home) & 7)]
    rev = lax.rem(NZ - z, NZ)

    def pick_row(x, r):
        return jnp.sum(jnp.where(row == r, x, 0), axis=0, keepdims=True)

    onward = dev(lax.rem(z + 1 - 2 * core + NZ, NZ) * 2 + core)

    def hop(h, t):
        return remote(
            stg[h].at[t], rcv[h].at[t], v.hop_send.at[h], v.hop_recv.at[h, t], onward
        )

    def sib_all(h):
        return whole(oth[h], v.sib_send.at[h], v.sib_recv.at[h])

    def take(h, t):
        hop(h, t).wait_recv()
        remote(rcv[h].at[t], oth[h].at[t], v.sib_send.at[h], v.sib_recv.at[h], sib).start()
        pool[h][CHIP + t] = rcv[h][t]

    def round_of(h, t):
        if t == 0:
            chip_copy(h).wait_recv()
        if t >= LAG:
            take(h, t - LAG)
        chosen = v.first_tab[0, t] if h == 0 and t < LAG else v.tab[1, t]
        stg[h][t] = pool[h][chosen]
        hop(h, t).start()

    for t in range(LAG):
        rings = [step(s, t) for s in rings]

    def my_picks():
        picks = jnp.where(core == 0, pick_row(rings[0][3], z), pick_row(rings[1][3], rev))
        return jnp.broadcast_to(picks, (8, 128))

    v.first_work[...] = my_picks()
    to_first = pltpu.make_async_copy(v.first_work, v.first_tab, v.misc.at[5])
    to_first.start()
    to_first.wait()
    for t in range(LAG):
        round_of(0, t)
    for t in range(LAG, SLOTS):
        rings = [step(s, t) for s in rings]
    over = jnp.maximum(rings[0][0], rings[1][0])
    over = jnp.max(jnp.max(over, axis=1, keepdims=True), axis=0, keepdims=True)
    v.flag_own[...] = jnp.broadcast_to(over, (8, 128))

    here = (z - home1 + 16) & 7
    loc_up = pick_row(rings[0][2], z)
    loc_down = pick_row(rings[1][2], rev)
    code = jnp.where(
        here == 0,
        lane1 & (CHIP - 1),
        jnp.where(here <= up, loc_up + SLOTS * core, loc_down + SLOTS * (1 - core)),
    )
    v.work[...] = my_picks()
    v.work[pl.ds(0, 1), :] = code
    to_scalars = pltpu.make_async_copy(v.work, v.tab, v.misc.at[2])
    to_scalars.start()

    def send_flag(j, d):
        remote(v.flag_own, v.flag_all.at[j - 1], v.misc.at[3], v.misc.at[4], (d, mem)).start()

    dp_peers(send_flag)
    to_scalars.wait()

    def prepare(h):
        sib_all(h).wait_recv()
        for j in range(TOPB):
            spot = v.tab[0, idx[0, 0, j]]
            here_kv = pool[h][jnp.minimum(spot, CHIP + SLOTS - 1)]
            there_kv = oth[h][jnp.clip(spot - CHIP - SLOTS, 0, SLOTS - 1)]
            both = jnp.where(spot < CHIP + SLOTS, here_kv, there_kv)
            place(j, both[0], both[1])

    half = SLOTS // 2
    order = []
    upcoming = [LAG, 0, 0, 0]

    def put(h):
        if h < KVH and upcoming[h] < SLOTS:
            order.append((h, upcoming[h]))
            upcoming[h] += 1

    for h in (0, 0, 1) * 3:
        put(h)
    for h in range(KVH):
        while upcoming[h] < SLOTS:
            put(h)
            put(h + 1)
    work = [functools.partial(project, 2), functools.partial(project, 3)]
    work += [functools.partial(transposes, n) for n in range(4)] + [ready]
    due = {}
    for n, (h, t) in enumerate(order):
        if t == SLOTS - 1 and h < KVH - 1:
            for i in range(LAG):
                due.setdefault(n + 1 + i, []).append(functools.partial(take, h, SLOTS - LAG + i))
            chunks = [functools.partial(prepare, h)]
            chunks += [functools.partial(part, h, i) for i in range(4)]
            chunks += [functools.partial(dp_start, h)]
            if h == 2:
                chunks += [functools.partial(dp_finish, 0, v.za_send, 0)]
            due.setdefault(n + (5 if h == 2 else 6), []).append(functools.partial(work.extend, chunks))
    for n, (h, t) in enumerate(order):
        round_of(h, t)
        for action in due.pop(n, []):
            action()
        if work and (n % 2 == 1 or n < half or h == 3 and t >= half):
            work.pop(0)()
    for t in range(SLOTS - LAG, SLOTS):
        if work:
            work.pop(0)()
        take(3, t)
    for n in sorted(due):
        for action in due[n]:
            action()
    while work:
        work.pop(0)()
    prepare(3)
    for n in range(4):
        part(3, n)
    dp_start(3)
    dp_finish(1, v.za_send, 1)
    dp_finish(2, v.za_send, 2)
    z_start(0, v.za_send, v.za_recv)
    grad_tokens()
    z_finish(0, v.za_send, v.za_recv, (0, 1, 2))
    dp_finish(3, v.zb_send, 0)
    z_start(1, v.zb_send, v.zb_recv)
    z_finish(1, v.zb_send, v.zb_recv, (3,))
    sent_all()
    z_all(1, v.zb_recv).wait_send()
    dp_seen = whole(v.flag_all, v.misc.at[3], v.misc.at[4])
    dp_seen.wait_recv()
    flag[...] = jnp.maximum(v.flag_own[...], jnp.max(v.flag_all[...], axis=0))
    for h in range(KVH):
        chip_copy(h).wait_send()
        whole(rcv[h], v.hop_send.at[h], v.hop_recv.at[h, 0]).wait_send()
    idx_seen.wait_send()
    dp_seen.wait_send()


def call(fast, args):
    hbm = pl.BlockSpec(memory_space=pl.ANY)
    vmem = pltpu.VMEM
    outs = [
        vmem((SEG, QW), BF16),
        vmem((SEG, D), BF16),
        vmem((D // (NDP * NMEM), QW), F32),
    ]
    if fast:
        outs.append(vmem((8, 128), I32))
    return pl.pallas_call(
        functools.partial(kernel, fast),
        out_shape=outs,
        in_specs=[hbm, hbm, hbm, hbm, pl.BlockSpec(memory_space=pltpu.SMEM), hbm],
        out_specs=[pl.BlockSpec(memory_space=vmem)] * len(outs),
        scratch_shapes=list((fast_scratch() if fast else slow_scratch()).values()),
        compiler_params=pltpu.CompilerParams(
            collective_id=0 if fast else 1,
            has_side_effects=True,
            vmem_limit_bytes=(58 if fast else 52) * 1024 * 1024,
        ),
    )(*args)


def store(*refs):
    copies = [
        pltpu.make_async_copy(src, dst, refs[6].at[i])
        for i, (src, dst) in enumerate(zip(refs[:3], refs[3:6]))
    ]
    for c in copies:
        c.start()
    for c in copies:
        c.wait()


def on_device(*args):
    ctx, gt, gw, flag = call(True, args)
    outs = lax.cond(flag[0, 0] > 0, lambda: tuple(call(False, args)), lambda: (ctx, gt, gw))
    hbm = pl.BlockSpec(memory_space=pl.ANY)
    return pl.pallas_call(
        store,
        out_shape=[jax.ShapeDtypeStruct(x.shape, x.dtype) for x in outs],
        in_specs=[hbm] * 3,
        out_specs=[hbm] * 3,
        scratch_shapes=[pltpu.SemaphoreType.DMA((3,))],
    )(*outs)


def solution(mesh):
    return jax.shard_map(
        on_device,
        mesh=mesh,
        in_specs=(
            P(("dp", "mem"), None),
            P(),
            P("dp", "mem", None, None),
            P("dp", "mem", None, None),
            P("dp", "mem", None),
            P(("dp", "mem"), None),
        ),
        out_specs=(P(("dp", "mem"), None), P(("dp", "mem"), None), P(("dp", "mem"), None)),
        check_vma=False,
    )
```
